256 devices in a mesh: loop: 128 (over y_hi, x, z, core), sub: 2 (over y_lo).
Axes of the slice: x: 4, y: 4 (y_hi: 2, y_lo: 2; y = y_hi * 2 + y_lo), z: 8, core: 2. Of those that a mesh axis runs over, the one named last changes fastest.
Arguments:
- embeddings: bfloat16 [65536, 1024], P(('loop', 'sub')), may hold values from -10 to 10
- reward: float32 [65536], P(('loop', 'sub')), may hold values from 0.5 to 13.5
- partner: int32 [65536], P(('loop', 'sub')), may hold values from 0 to 65535, as said below
- policy: int32 [65536], P(('loop', 'sub')), may hold values from 0 to 15
Outputs:
- weighted_loss: float32 [65536], P(('loop', 'sub'))
- gradient: float32 [65536, 1024], P(('loop', 'sub'))
- policy_loss: float32 [16], replicated
The draws below stay inside these ranges and needn't reach their ends.
Inputs may be any that keep to these rules, and one draw needn't show every extreme that they name: partner_i is a view other than i in the same block of 512 views, and partner of partner_i is i.
All inputs are finite; a program needn't handle non-finite values.
Results may differ from the reference program's by a relative error of at most 0.0029.
Values may be sent and summed in bfloat16 or wider, within the bound.
A program may use at most 64 MiB of HBM per device.

```python
import math
import jax
import jax.numpy as jnp
from jax import lax

D = 1024
RADIUS = 4
POLICIES = 16
BLOCK = 512
VIEWS = 65536
N_LOOP = 128


def draw_embeddings(key, part):
    key = jax.random.fold_in(key, 11)
    first_key, second_key = jax.random.split(key, 2)
    drawn = jnp.clip(jax.random.normal(first_key, (VIEWS, D), jnp.float32), -4.0, 4.0)
    row_scale = jnp.exp(jax.random.uniform(second_key, (VIEWS, 1), jnp.float32, math.log(0.5), math.log(2.5)))
    result = drawn * row_scale
    return result.astype(jnp.bfloat16)


def draw_reward(key, part):
    key = jax.random.fold_in(key, 7)
    position = jnp.arange(VIEWS, dtype=jnp.float32) / max(VIEWS - 1, 1)
    base = jax.random.uniform(key, (VIEWS,), jnp.float32, 0.5, 1.5)
    result = base * (1.0 + 2.0 * position)
    return result


def draw_partner(key, part):
    key = jax.random.fold_in(key, 5)
    block_count = VIEWS // BLOCK

    def one_block(block_key):
        order = jax.random.permutation(block_key, BLOCK).astype(jnp.int32)
        first_half = order[0::2]
        second_half = order[1::2]
        paired = jnp.zeros((BLOCK,), jnp.int32).at[first_half].set(second_half)
        return paired.at[second_half].set(first_half)
    block_keys = jax.random.split(key, block_count)
    paired_local = jax.vmap(one_block)(block_keys)
    starts = (jnp.arange(block_count, dtype=jnp.int32) * BLOCK)[:, None]
    return (paired_local + starts).reshape(VIEWS).astype(jnp.int32)


def touch_ends(entries, key, least, largest):
    longest = entries.shape.index(max(entries.shape))
    spots = []
    for shift in (0, 1):
        where = [jax.random.randint(jax.random.fold_in(key, axis), (), 0, length) for axis, length in enumerate(entries.shape)]
        where[longest] = (where[longest] + shift) % entries.shape[longest]
        spots.append(tuple(where))
    return entries.at[spots[0]].set(least).at[spots[1]].set(largest)


def setup_inputs(seed: int = 0) -> dict:
    splits = jax.random.split(jax.random.key(seed), 5)
    return {
        "embeddings": draw_embeddings(jax.random.fold_in(splits[4], 71), 0),
        "reward": draw_reward(jax.random.fold_in(splits[4], 71), 0),
        "partner": draw_partner(jax.random.fold_in(splits[4], 71), 0),
        "policy": touch_ends(jax.random.randint(splits[3], (VIEWS,), 0, POLICIES), jax.random.fold_in(splits[3], 1), 0, POLICIES - 1).astype(jnp.int32),
    }


def reference(embeddings, reward, partner, policy):
    blocks = embeddings.reshape(N_LOOP, BLOCK, D)
    offset_list = [0] + [-step for step in range(1, RADIUS + 1)] + [step for step in range(1, RADIUS + 1)]
    offsets = jnp.array(offset_list, dtype=jnp.int32)
    factor = 1.0 / math.sqrt(D)
    block_ids = jnp.arange(N_LOOP, dtype=jnp.int32)
    width_keys = (2 * RADIUS + 1) * BLOCK
    columns = jnp.arange(width_keys, dtype=jnp.int32)
    self_mask = columns[None, :] == jnp.arange(BLOCK, dtype=jnp.int32)[:, None]

    def scores_of(block_id):
        queries = lax.dynamic_index_in_dim(blocks, block_id, 0, keepdims=False)
        neighbour_ids = (block_id + offsets) % N_LOOP
        key_rows = jnp.take(blocks, neighbour_ids, axis=0).reshape(width_keys, D)
        scores = jnp.dot(queries, key_rows.T, preferred_element_type=jnp.float32) * factor
        scores = jnp.where(self_mask, -jnp.inf, scores)
        return (scores, key_rows, neighbour_ids)

    def first_pass(block_id):
        scores, key_rows, neighbour_ids = scores_of(block_id)
        row_max = lax.optimization_barrier(jnp.max(scores, axis=1))
        return row_max + jnp.log(lax.optimization_barrier(jnp.sum(jnp.exp(scores - row_max[:, None]), axis=1)))
    log_total = lax.map(first_pass, block_ids)
    reward_blocks = reward.reshape(N_LOOP, BLOCK)
    partner_local = partner.reshape(N_LOOP, BLOCK) - block_ids[:, None] * BLOCK

    def second_pass(block_id):
        scores, key_rows, neighbour_ids = scores_of(block_id)
        own_total = lax.dynamic_index_in_dim(log_total, block_id, 0, keepdims=False)
        own_reward = lax.dynamic_index_in_dim(reward_blocks, block_id, 0, keepdims=False)
        own_partner = lax.dynamic_index_in_dim(partner_local, block_id, 0, keepdims=False)
        key_total = jnp.take(log_total, neighbour_ids, axis=0).reshape(width_keys)
        key_reward = jnp.take(reward_blocks, neighbour_ids, axis=0).reshape(width_keys)
        matched = columns[None, :] == own_partner[:, None]
        positive = lax.optimization_barrier(jnp.sum(jnp.where(matched, scores, 0.0), axis=1))
        weighted = own_reward * (own_total - positive)
        partner_weight = lax.optimization_barrier(jnp.sum(jnp.where(matched, key_reward[None, :], 0.0), axis=1))
        coefficient = own_reward[:, None] * jnp.exp(scores - own_total[:, None]) + key_reward[None, :] * jnp.exp(scores - key_total[None, :])
        coefficient = coefficient - jnp.where(matched, (own_reward + partner_weight)[:, None], 0.0)
        coefficient = coefficient.astype(jnp.bfloat16)
        gradient = jnp.dot(coefficient, key_rows, preferred_element_type=jnp.float32)
        return (weighted, gradient)
    weighted, gradient = lax.map(second_pass, block_ids)
    weighted_loss = weighted.reshape(VIEWS)
    gradient = gradient.reshape(VIEWS, D)
    labels = policy[:, None] == jnp.arange(POLICIES, dtype=jnp.int32)[None, :]
    policy_loss = lax.optimization_barrier(jnp.sum(jnp.where(labels, weighted_loss[:, None], 0.0), axis=0)) * (POLICIES / VIEWS)
    return (weighted_loss, gradient, policy_loss)
```

```python
import functools
import math

import jax
import jax.numpy as jnp
from jax import lax
from jax.experimental import pallas as pl
from jax.experimental.pallas import tpu as pltpu
from jax.sharding import PartitionSpec as P

RADIUS = 4
POLICIES = 16
ROWS = 256
WIDTH = 1024
SUBS = 2
BLOCK = ROWS * SUBS
LOOP = 128
SEAM = 64
CHUNKS = 4
TILE = 256
PART = ROWS // CHUNKS
SLOTS = (2 * RADIUS + 1) * SUBS
GROUP = 16
LOG2E = 1.4426950408889634
LN2 = 0.6931471805599453
LOWEST = -1e30
MESH = pl.DeviceIdType.MESH

LOW_OWN, LOW_HALF, LOW_FAR, UP_OWN, UP_HALF, UP_FAR, SUB_OWN, SUB_LOW, SUB_UP = range(9)
CORE_OWN, CORE_HALF, CORE_LOW_A, CORE_LOW_B, CORE_UP_A, CORE_UP_B, CORE_FAR_A, CORE_FAR_B = range(9, 17)
CLASSES = 17


def slot(offset, half):
    return (offset + RADIUS) * SUBS + half


def kernel(
    x_ref, reward_ref, partner_ref, policy_ref,
    weighted_ref, gradient_ref, loss_ref,
    keys, scores, weights, level, rewards, first_sum, second_sum,
    recv, send, level_sem, sum_sem, reward_sem, local_sem,
):
    block = lax.axis_index("loop")
    sub = lax.axis_index("sub")
    core = lax.rem(block, 2)

    def crosses(at):
        return jnp.where(lax.rem(at, SEAM) >= SEAM - 2, 1, 0)

    def flip(half, by):
        return half + by - 2 * half * by

    def at_loop(index):
        return lax.rem(index + LOOP, LOOP)

    cross_up = crosses(block)
    cross_low = crosses(at_loop(block - 2))
    cross_up2 = crosses(at_loop(block + 2))
    cross_low2 = crosses(at_loop(block - 4))
    up_dev = (at_loop(block + 2), flip(sub, cross_up))
    low_dev = (at_loop(block - 2), flip(sub, cross_low))
    sub_dev = (block, 1 - sub)
    core_dev = (block + 1 - 2 * core, sub)
    low_half = flip(sub, cross_low)
    up_half = flip(sub, cross_up)
    low_far = flip(low_half, cross_low2)
    up_far = flip(up_half, cross_up2)

    own_slot = slot(0, sub)
    half_slot = slot(0, 1 - sub)

    def piece(index):
        return pl.ds(pl.multiple_of(index * ROWS, ROWS), ROWS)

    load = pltpu.make_async_copy(x_ref, keys.at[piece(own_slot)], local_sem)
    load.start()

    targets = [up_dev, low_dev, sub_dev, core_dev]
    level_targets = []
    for offset in range(-RADIUS, RADIUS + 1):
        for other in range(SUBS):
            if offset == 0 and other == 0:
                continue
            level_targets.append((offset, (at_loop(block + offset), flip(sub, other))))
    line = lax.rem(block, GROUP)
    line_base = block - line
    first_targets = [(line_base + lax.rem(line + i, GROUP), sub) for i in range(1, GROUP)]
    plane = (block // GROUP) * SUBS + sub
    second_targets = []
    for i in range(1, GROUP):
        other = lax.rem(plane + i, GROUP)
        second_targets.append(((other // SUBS) * GROUP + line, lax.rem(other, SUBS)))
    barrier = pltpu.get_barrier_semaphore()
    everybody = targets + [t for _, t in level_targets] + first_targets + second_targets
    for device in everybody:
        pl.semaphore_signal(barrier, inc=1, device_id=device, device_id_type=MESH)
    load.wait()
    pl.semaphore_wait(barrier, len(everybody))

    def rows(index, q):
        return pl.ds(pl.multiple_of(index * ROWS + q * PART, PART), PART)

    def push(source, target, kind, q, link, device):
        pltpu.make_async_remote_copy(
            src_ref=keys.at[rows(source, q)],
            dst_ref=keys.at[rows(target, q)],
            send_sem=send.at[link],
            recv_sem=recv.at[kind, q],
            device_id=device,
            device_id_type=MESH,
        ).start()

    def await_piece(kind, q):
        ref = keys.at[pl.ds(0, PART)]
        pltpu.make_async_copy(ref, ref, recv.at[kind, q]).wait()

    UP, LOW, SUB, CORE = range(4)
    shift = 2 * core - 1

    def to_core(offset, half, kind, q):
        push(slot(offset, half), slot(offset + shift, half), kind, q, CORE, core_dev)

    def send_own(q):
        push(own_slot, slot(-2, sub), LOW_OWN, q, UP, up_dev)
        push(own_slot, slot(2, sub), UP_OWN, q, LOW, low_dev)

    def send_half(q):
        push(half_slot, slot(-2, 1 - sub), LOW_HALF, q, UP, up_dev)
        push(half_slot, slot(2, 1 - sub), UP_HALF, q, LOW, low_dev)

    def send_far(q):
        push(slot(-2, low_half), slot(-4, low_half), LOW_FAR, q, UP, up_dev)
        push(slot(2, up_half), slot(4, up_half), UP_FAR, q, LOW, low_dev)

    def got_own(q):
        await_piece(LOW_OWN, q)
        await_piece(UP_OWN, q)
        send_far(q)

    def spread_own(q):
        to_core(-2, low_half, CORE_LOW_A, q)
        to_core(2, up_half, CORE_UP_A, q)

    def got_half(q):
        await_piece(SUB_OWN, q)
        to_core(0, 1 - sub, CORE_HALF, q)

    far_offset = 4 - 8 * core
    far_half = up_far + core * (low_far - up_far)

    def got_far(q):
        await_piece(LOW_FAR, q)
        await_piece(UP_FAR, q)
        push(slot(-4, low_far), slot(-4, low_far), SUB_LOW, q, SUB, sub_dev)
        push(slot(4, up_far), slot(4, up_far), SUB_UP, q, SUB, sub_dev)
        to_core(far_offset, far_half, CORE_FAR_A, q)

    def got_near(q):
        await_piece(LOW_HALF, q)
        await_piece(UP_HALF, q)
        to_core(-2, 1 - low_half, CORE_LOW_B, q)
        to_core(2, 1 - up_half, CORE_UP_B, q)

    def got_sub(q):
        await_piece(SUB_LOW, q)
        await_piece(SUB_UP, q)
        to_core(far_offset, 1 - far_half, CORE_FAR_B, q)

    def await_all(kind):
        for q in range(CHUNKS):
            await_piece(kind, q)

    row_at = lax.broadcasted_iota(jnp.int32, (ROWS, ROWS), 0)
    column_at = lax.broadcasted_iota(jnp.int32, (ROWS, ROWS), 1)
    diagonal = row_at == column_at
    column_float = column_at.astype(jnp.float32)

    def as_column(row):
        return jnp.sum(jnp.where(diagonal, row, 0.0), axis=1, keepdims=True)

    def as_row(column):
        return jnp.sum(jnp.where(diagonal, column, 0.0), axis=0, keepdims=True)

    factor = LOG2E / math.sqrt(WIDTH)

    def score(index):
        return (
            lax.dot_general(
                keys[piece(own_slot), :], keys[piece(index), :], (((1,), (1,)), ((), ())),
                preferred_element_type=jnp.float32,
            )
            * factor
        )

    top = [None]
    total = [None]

    def absorb(index, own=False):
        tile = score(index)
        if own:
            tile = jnp.where(diagonal, LOWEST, tile)
        scores[index] = tile
        left, right = tile[:, :128], tile[:, 128:]
        high = jnp.maximum(left, right)
        if top[0] is None:
            top[0] = high
            total[0] = jnp.exp2(left - high) + jnp.exp2(right - high)
        else:
            high = jnp.maximum(high, top[0])
            total[0] = (
                total[0] * jnp.exp2(top[0] - high)
                + jnp.exp2(left - high)
                + jnp.exp2(right - high)
            )
            top[0] = high

    send_own(0)
    for q in range(CHUNKS):
        push(own_slot, own_slot, SUB_OWN, q, SUB, sub_dev)
        if q == 0:
            send_own(1)
    for q in range(CHUNKS):
        push(own_slot, slot(shift, sub), CORE_OWN, q, CORE, core_dev)

    reward_row = reward_ref[...]
    rewards[sub] = reward_row
    reward_copy = pltpu.make_async_remote_copy(
        src_ref=rewards.at[sub], dst_ref=rewards.at[sub],
        send_sem=reward_sem.at[0], recv_sem=reward_sem.at[1],
        device_id=sub_dev, device_id_type=MESH,
    )
    reward_copy.start()
    absorb(own_slot, own=True)
    reward_column = as_column(reward_row)
    partner_column = as_column((partner_ref[...] - block * BLOCK).astype(jnp.float32))
    policy_column = as_column(policy_ref[...].astype(jnp.float32))

    got_own(0)
    send_own(2)
    spread_own(0)
    got_half(0)
    await_all(CORE_OWN)
    absorb(slot(-shift, sub))

    got_own(1)
    send_own(3)
    spread_own(1)
    got_half(1)

    got_far(0)
    got_half(2)

    got_own(2)
    send_half(0)
    spread_own(2)
    got_half(3)
    absorb(half_slot)

    got_far(1)
    await_all(CORE_HALF)
    absorb(slot(-shift, 1 - sub))
    got_own(3)
    for q in range(1, CHUNKS):
        send_half(q)
    spread_own(3)
    got_sub(0)
    absorb(slot(-2, low_half))

    got_far(2)
    absorb(slot(2, up_half))
    got_near(0)
    await_all(CORE_LOW_A)
    await_all(CORE_UP_A)
    absorb(slot(-2 - shift, low_half))
    got_sub(1)
    absorb(slot(2 - shift, up_half))
    got_far(3)
    absorb(slot(-4, low_far))
    got_near(1)
    absorb(slot(4, up_far))
    got_sub(2)
    core_far = -far_offset - shift
    core_far_half = low_far + core * (up_far - low_far)
    await_all(CORE_FAR_A)
    absorb(slot(core_far, core_far_half))
    got_near(2)
    got_near(3)
    got_sub(3)
    absorb(slot(-2, 1 - low_half))
    absorb(slot(2, 1 - up_half))
    absorb(slot(-4, 1 - low_far))
    absorb(slot(4, 1 - up_far))
    await_all(CORE_LOW_B)
    absorb(slot(-2 - shift, 1 - low_half))
    await_all(CORE_UP_B)
    absorb(slot(2 - shift, 1 - up_half))
    await_all(CORE_FAR_B)
    absorb(slot(core_far, 1 - core_far_half))

    peak = jnp.max(top[0], axis=1, keepdims=True)
    summed = jnp.sum(total[0] * jnp.exp2(top[0] - peak), axis=1, keepdims=True)
    log_total = peak + jnp.log(summed) * LOG2E
    own_level = log_total - jnp.log(reward_column) * LOG2E
    level[own_slot] = as_row(own_level)
    for offset, device in level_targets:
        pltpu.make_async_remote_copy(
            src_ref=level.at[own_slot],
            dst_ref=level.at[slot(-offset, sub)],
            send_sem=level_sem.at[0],
            recv_sem=level_sem.at[1],
            device_id=device,
            device_id_type=MESH,
        ).start()

    own_match = column_float + (sub * ROWS).astype(jnp.float32) == partner_column
    half_match = column_float + ((1 - sub) * ROWS).astype(jnp.float32) == partner_column
    positive = jnp.sum(
        jnp.where(own_match, scores[own_slot], 0.0)
        + jnp.where(half_match, scores[half_slot], 0.0),
        axis=1, keepdims=True,
    )
    weighted = reward_column * ((log_total - positive) * LN2)
    weighted_ref[...] = as_row(weighted)
    labels = lax.broadcasted_iota(jnp.int32, (ROWS, 128), 1).astype(jnp.float32)
    first_sum[line] = jnp.sum(
        jnp.where(labels == policy_column, weighted, 0.0), axis=0, keepdims=True
    )
    for device in first_targets:
        pltpu.make_async_remote_copy(
            src_ref=first_sum.at[line], dst_ref=first_sum.at[line],
            send_sem=sum_sem.at[0], recv_sem=sum_sem.at[1],
            device_id=device, device_id_type=MESH,
        ).start()

    def await_rows(ref, count, sem):
        part = ref.at[pl.ds(0, count)]
        pltpu.make_async_copy(part, part, sem).wait()

    await_rows(level, SLOTS - 1, level_sem.at[1])
    reward_copy.wait()

    for index in range(SLOTS):
        tile = scores[index]
        value = jnp.exp2(tile - own_level) + jnp.exp2(tile - level[index])
        half = index - slot(0, 0)
        if 0 <= half < SUBS:
            match = column_float + float(half * ROWS) == partner_column
            value = value - jnp.where(match, reward_column + rewards[half], 0.0)
        weights[:, index * ROWS : (index + 1) * ROWS] = value.astype(jnp.bfloat16)

    await_rows(first_sum, GROUP - 1, sum_sem.at[1])
    second_sum[plane] = jnp.sum(first_sum[...], axis=0)
    for device in second_targets:
        pltpu.make_async_remote_copy(
            src_ref=second_sum.at[plane], dst_ref=second_sum.at[plane],
            send_sem=sum_sem.at[2], recv_sem=sum_sem.at[3],
            device_id=device, device_id_type=MESH,
        ).start()

    for tile in range(WIDTH // TILE):
        columns = pl.ds(tile * TILE, TILE)
        gradient_ref[:, columns] = jnp.dot(
            weights[...], keys[:, columns], preferred_element_type=jnp.float32
        )

    await_rows(second_sum, GROUP - 1, sum_sem.at[3])
    loss_ref[...] = jnp.sum(second_sum[...], axis=0) * (POLICIES / (LOOP * BLOCK))

    await_rows(level, SLOTS - 1, level_sem.at[0])
    await_rows(first_sum, GROUP - 1, sum_sem.at[0])
    await_rows(second_sum, GROUP - 1, sum_sem.at[2])
    for link, pieces in ((UP, 3), (LOW, 3), (SUB, 3), (CORE, 8)):
        part = keys.at[pl.ds(0, pieces * ROWS)]
        pltpu.make_async_copy(part, part, send.at[link]).wait()


def body(embeddings, reward, partner, policy):
    vmem = pl.BlockSpec(memory_space=pltpu.VMEM)
    weighted, gradient, loss = pl.pallas_call(
        kernel,
        out_shape=(
            jax.ShapeDtypeStruct((1, ROWS), jnp.float32),
            jax.ShapeDtypeStruct((ROWS, WIDTH), jnp.float32),
            jax.ShapeDtypeStruct((1, 128), jnp.float32),
        ),
        in_specs=[pl.BlockSpec(memory_space=pl.ANY), vmem, vmem, vmem],
        out_specs=(vmem, vmem, vmem),
        scratch_shapes=[
            pltpu.VMEM((SLOTS * ROWS, WIDTH), jnp.bfloat16),
            pltpu.VMEM((SLOTS, ROWS, ROWS), jnp.float32),
            pltpu.VMEM((ROWS, SLOTS * ROWS), jnp.bfloat16),
            pltpu.VMEM((SLOTS, 1, ROWS), jnp.float32),
            pltpu.VMEM((SUBS, 1, ROWS), jnp.float32),
            pltpu.VMEM((GROUP, 1, 128), jnp.float32),
            pltpu.VMEM((GROUP, 1, 128), jnp.float32),
            pltpu.SemaphoreType.DMA((CLASSES, CHUNKS)),
            pltpu.SemaphoreType.DMA((4,)),
            pltpu.SemaphoreType.DMA((2,)),
            pltpu.SemaphoreType.DMA((4,)),
            pltpu.SemaphoreType.DMA((2,)),
            pltpu.SemaphoreType.DMA,
        ],
        name="band",
        compiler_params=pltpu.CompilerParams(
            collective_id=0, has_side_effects=True, vmem_limit_bytes=48 * 2**20
        ),
    )(
        embeddings,
        reward.reshape(1, ROWS),
        partner.reshape(1, ROWS),
        policy.reshape(1, ROWS),
    )
    return weighted.reshape(ROWS), gradient, loss[0, :POLICIES]


def solution(mesh):
    rows = P(("loop", "sub"))
    matrix = P(("loop", "sub"), None)
    return jax.shard_map(
        body, mesh=mesh, in_specs=(matrix, rows, rows, rows),
        out_specs=(rows, matrix, P()), check_vma=False,
    )
```

```python
import functools
import math

import jax
import jax.numpy as jnp
from jax import lax
from jax.experimental import pallas as pl
from jax.experimental.pallas import tpu as pltpu
from jax.sharding import PartitionSpec as P

RADIUS = 4
POLICIES = 16
ROWS = 256
WIDTH = 1024
SUBS = 2
BLOCK = ROWS * SUBS
LOOP = 128
SEAM = 64
CHUNKS = 8
LINE = 8
MOVED = 2
SPAN = 3
LEVELS = 2 * RADIUS + 1
PIECES = 4
PART = ROWS // CHUNKS
SLOTS = (2 * RADIUS + 1) * SUBS
GROUP = 16
LOG2E = 1.4426950408889634
LN2 = 0.6931471805599453
LOWEST = -1e30
MESH = pl.DeviceIdType.MESH

OWN, HALF, FAR, SUB_FAR = 0, 2, 4, 6
CORE_NEAR_A, CORE_NEAR_B = 8, 10
SUB_OWN, CORE_OWN, CORE_HALF, CORE_FAR_A, CORE_FAR_B = 12, 13, 14, 15, 16
CLASSES = 17


def slot(offset, half):
    return (offset + RADIUS) * SUBS + half


def kernel(
    x_ref, reward_ref, partner_ref, policy_ref,
    weighted_ref, gradient_ref, loss_ref,
    keys, scores, shares, level, rewards, integers, first_sum, second_sum,
    recv, send, level_sem, sum_sem, reward_sem, local_sem,
):
    block = lax.axis_index("loop")
    sub = lax.axis_index("sub")
    core = lax.rem(block, 2)

    def crosses(at):
        return jnp.where(lax.rem(at, SEAM) >= SEAM - 2, 1, 0)

    def flip(half, by):
        return half + by - 2 * half * by

    def at_loop(index):
        return lax.rem(index + LOOP, LOOP)

    cross_up = crosses(block)
    cross_low = crosses(at_loop(block - 2))
    cross_up2 = crosses(at_loop(block + 2))
    cross_low2 = crosses(at_loop(block - 4))
    up_dev = (at_loop(block + 2), flip(sub, cross_up))
    low_dev = (at_loop(block - 2), flip(sub, cross_low))
    sub_dev = (block, 1 - sub)
    core_dev = (block + 1 - 2 * core, sub)
    low_half = flip(sub, cross_low)
    up_half = flip(sub, cross_up)
    low_far = flip(low_half, cross_low2)
    up_far = flip(up_half, cross_up2)

    own_slot = slot(0, sub)
    half_slot = slot(0, 1 - sub)

    def piece(index):
        return pl.ds(pl.multiple_of(index * ROWS, ROWS), ROWS)

    loads = [
        pltpu.make_async_copy(x_ref, keys.at[piece(own_slot)], local_sem.at[0]),
        pltpu.make_async_copy(reward_ref, rewards.at[sub], local_sem.at[1]),
        pltpu.make_async_copy(partner_ref, integers.at[0], local_sem.at[2]),
        pltpu.make_async_copy(policy_ref, integers.at[1], local_sem.at[3]),
    ]
    for load in loads:
        load.start()

    level_targets = []
    for offset in sorted(range(-RADIUS, RADIUS + 1), key=lambda k: (k % 2, abs(k))):
        for other in range(SUBS):
            if offset == 0 and other == 0:
                continue
            level_targets.append((offset, (at_loop(block + offset), flip(sub, other))))
    line = lax.rem(block, GROUP)
    line_base = block - line
    first_targets = [(line_base + lax.rem(line + i, GROUP), sub) for i in range(1, GROUP)]
    plane = (block // GROUP) * SUBS + sub
    second_targets = []
    for i in range(1, GROUP):
        other = lax.rem(plane + i, GROUP)
        second_targets.append(((other // SUBS) * GROUP + line, lax.rem(other, SUBS)))
    barrier = pltpu.get_barrier_semaphore()
    everybody = [t for _, t in level_targets] + first_targets + second_targets
    for device in everybody:
        pl.semaphore_signal(barrier, inc=1, device_id=device, device_id_type=MESH)
    for load in loads:
        load.wait()
    pl.semaphore_wait(barrier, len(everybody))

    def rows(index, q):
        return pl.ds(pl.multiple_of(index * ROWS + q * PART, PART), PART)

    def push(source, target, kind, q, link, device):
        pltpu.make_async_remote_copy(
            src_ref=keys.at[rows(source, q)],
            dst_ref=keys.at[rows(target, q)],
            send_sem=send.at[link],
            recv_sem=recv.at[kind, q],
            device_id=device,
            device_id_type=MESH,
        ).start()

    def await_piece(kind, q):
        ref = keys.at[pl.ds(0, PART)]
        pltpu.make_async_copy(ref, ref, recv.at[kind, q]).wait()

    SUB, CORE = 2, 3
    shift = 2 * core - 1

    z = lax.rem(block // 2, LINE)
    side_b = jnp.where(z >= LINE // 2, 1, 0)
    side_a = 1 - side_b
    edge = jnp.where(jnp.logical_or(z < 2, z >= LINE - 2), 1, 0)

    def pick(side, low, up):
        return low + side * (up - low)

    def near(side):
        return 4 * side - 2

    def device_of(side):
        return tuple(pick(side, low, up) for low, up in zip(low_dev, up_dev))

    def near_half(side):
        return pick(side, low_half, up_half)

    def far_half_of(side):
        return pick(side, low_far, up_far)

    def to_core(offset, half, kind, q):
        push(slot(offset, half), slot(offset + shift, half), kind, q, CORE, core_dev)

    def send_own(side, *chunks):
        for q in chunks:
            push(own_slot, slot(-near(side), sub), OWN + 1 - side, q, side, device_of(side))

    def send_half(side, *chunks):
        for q in chunks:
            push(
                half_slot, slot(-near(side), 1 - sub), HALF + 1 - side, q, side,
                device_of(side),
            )

    def got_own(side, q):
        other = 1 - side
        await_piece(OWN + side, q)
        half = near_half(side)
        push(
            slot(near(side), half), slot(-2 * near(other), half), FAR + side, q, other,
            device_of(other),
        )

    def spread_own(side, q):
        to_core(near(side), near_half(side), CORE_NEAR_A + side, q)

    def got_half(q):
        await_piece(SUB_OWN, q)
        to_core(0, 1 - sub, CORE_HALF, q)

    far_offset = 4 - 8 * core
    far_half = far_half_of(1 - core)

    def got_far(side, q):
        await_piece(FAR + side, q)
        at = slot(2 * near(side), far_half_of(side))
        push(at, at, SUB_FAR + side, q, SUB, sub_dev)

    def spread_far(q):
        to_core(far_offset, far_half, CORE_FAR_A, q)

    def got_near(side, q):
        await_piece(HALF + side, q)
        to_core(near(side), 1 - near_half(side), CORE_NEAR_B + side, q)

    def got_sub(q):
        await_piece(SUB_FAR, q)
        await_piece(SUB_FAR + 1, q)
        to_core(far_offset, 1 - far_half, CORE_FAR_B, q)

    def await_all(kind):
        for q in range(CHUNKS):
            await_piece(kind, q)

    row_at = lax.broadcasted_iota(jnp.int32, (ROWS, ROWS), 0)
    column_at = lax.broadcasted_iota(jnp.int32, (ROWS, ROWS), 1)
    diagonal = row_at == column_at
    column_float = column_at.astype(jnp.float32)

    def as_column(row):
        return jnp.sum(jnp.where(diagonal, row, 0.0), axis=1, keepdims=True)

    def as_row(column):
        return jnp.sum(jnp.where(diagonal, column, 0.0), axis=0, keepdims=True)

    factor = LOG2E / math.sqrt(WIDTH)

    top = [None]
    total = [None]

    def absorb(index, part=None, own=False):
        absorb_all([index], part, own)

    def absorb_all(indices, part=None, own=False):
        first, count = (0, ROWS) if part is None else (part * 128, 128)
        parts = []
        for index in indices:
            block_rows = pl.ds(pl.multiple_of(index * ROWS + first, 128), count)
            tile = lax.dot_general(
                keys[piece(own_slot), :], keys[block_rows, :], (((1,), (1,)), ((), ())),
                preferred_element_type=jnp.float32,
            ) * factor
            if own:
                tile = jnp.where(diagonal, LOWEST, tile)
            scores[index, :, first : first + count] = tile
            parts += [tile[:, i : i + 128] for i in range(0, count, 128)]
        high = functools.reduce(jnp.maximum, parts)
        if top[0] is not None:
            high = jnp.maximum(high, top[0])
        fresh = functools.reduce(jnp.add, [jnp.exp2(t - high) for t in parts])
        if top[0] is not None:
            fresh = fresh + total[0] * jnp.exp2(top[0] - high)
        top[0], total[0] = high, fresh

    for q in range(4):
        send_own(side_a, q)
        send_own(side_b, q)
        push(own_slot, own_slot, SUB_OWN, q, SUB, sub_dev)

    @pl.when(edge == 1)
    def _():
        send_own(side_a, 4, 5)

    for q in range(4, CHUNKS):
        push(own_slot, own_slot, SUB_OWN, q, SUB, sub_dev)

    def near_a(q):
        got_own(side_a, q)
        if q < 4:
            send_own(side_b, q + 4)
        elif q < 7:
            send_half(side_b, q - 4)
        else:
            send_half(side_b, *range(3, CHUNKS - MOVED))

            @pl.when(z != 0)
            def _():
                send_half(side_b, *range(CHUNKS - MOVED, CHUNKS))
        spread_own(side_a, q)

    def near_b(q):
        got_own(side_b, q)
        if q < 2:
            send_own(side_a, q + 4 + 2 * edge)
        elif q < 4:

            @pl.when(edge == 1)
            def _():
                send_half(side_a, q - 2)

            @pl.when(edge == 0)
            def _():
                send_own(side_a, q + 4)
        else:
            send_half(side_a, q - 4 + 2 * edge)
        if q == 7:

            @pl.when(edge == 0)
            def _():
                send_half(side_a, 4, 5)

            send_half(side_a, 6, 7)
        if q >= CHUNKS - MOVED:
            at = slot(near(side_b), near_half(side_b))

            @pl.when(z == LINE - 1)
            def _():
                push(at, at, HALF + side_b, q, SUB, sub_dev)
        spread_own(side_b, q)

    def far_a(q):
        got_far(side_a, q)

    def far_b(q):
        got_far(side_b, q)
        spread_far(q)

    near_a(0)
    for q in range(CHUNKS):
        push(own_slot, slot(shift, sub), CORE_OWN, q, CORE, core_dev)
    reward_copy = pltpu.make_async_remote_copy(
        src_ref=rewards.at[sub], dst_ref=rewards.at[sub],
        send_sem=reward_sem.at[0], recv_sem=reward_sem.at[1],
        device_id=sub_dev, device_id_type=MESH,
    )
    reward_copy.start()
    near_a(1)
    absorb(own_slot, own=True)
    near_a(2)
    near_b(0)
    near_a(3)
    near_b(1)
    far_a(0)
    for q in range(3):
        got_half(q)
    near_b(2)
    near_a(4)
    near_b(3)
    far_a(1)
    await_all(CORE_OWN)
    absorb(slot(-shift, sub))
    near_a(5)
    far_b(0)
    far_a(2)
    for q in range(3, CHUNKS):
        got_half(q)
    near_b(4)
    near_a(6)
    far_b(1)
    near_b(5)
    far_a(3)
    absorb(half_slot)
    near_a(7)
    far_b(2)
    near_b(6)
    far_a(4)
    reward_row = rewards[sub]
    reward_column = as_column(reward_row)
    partner_column = as_column((integers[0] - block * BLOCK).astype(jnp.float32))
    policy_column = as_column(integers[1].astype(jnp.float32))
    log_reward = jnp.log(reward_column) * LOG2E
    absorb(slot(near(side_a), near_half(side_a)))
    far_b(3)
    near_b(7)
    far_a(5)
    await_all(CORE_HALF)
    absorb(slot(-shift, 1 - sub))
    absorb(slot(near(side_b), near_half(side_b)))
    far_b(4)
    await_all(CORE_NEAR_A + side_a)
    absorb(slot(near(side_a) - shift, near_half(side_a)))
    far_a(6)
    await_all(CORE_NEAR_A + side_b)
    absorb(slot(near(side_b) - shift, near_half(side_b)))
    own_match = column_float + (sub * ROWS).astype(jnp.float32) == partner_column
    half_match = column_float + ((1 - sub) * ROWS).astype(jnp.float32) == partner_column
    positive = jnp.sum(
        jnp.where(own_match, scores[own_slot], 0.0)
        + jnp.where(half_match, scores[half_slot], 0.0),
        axis=1, keepdims=True,
    )
    far_b(5)
    absorb(slot(2 * near(side_a), far_half_of(side_a)), 0)
    far_a(7)
    absorb(slot(2 * near(side_b), far_half_of(side_b)), 0)
    for q in range(3):
        got_sub(q)
        got_near(side_a, q)
        got_near(side_b, q)
    far_b(6)
    absorb(slot(2 * near(side_a), far_half_of(side_a)), 1)
    core_far = -far_offset - shift
    core_far_half = far_half_of(core)
    got_sub(3)
    got_near(side_a, 3)
    got_near(side_b, 3)
    far_b(7)

    def await_some(kind, part):
        for q in range(part * CHUNKS // 2, (part + 1) * CHUNKS // 2):
            await_piece(kind, q)

    def rest(part):
        sides = (side_a, side_b)
        absorb_all(
            [slot(near(side), 1 - near_half(side)) for side in sides]
            + [slot(2 * near(side), 1 - far_half_of(side)) for side in sides],
            part,
        )
        for side in sides:
            await_some(CORE_NEAR_B + side, part)
        await_some(CORE_FAR_B, part)
        absorb_all(
            [slot(near(side) - shift, 1 - near_half(side)) for side in sides]
            + [slot(core_far, 1 - core_far_half)],
            part,
        )

    rest(0)
    absorb(slot(2 * near(side_b), far_half_of(side_b)), 1)
    await_all(CORE_FAR_A)
    absorb(slot(core_far, core_far_half))
    for q in range(4, CHUNKS):
        got_near(side_a, q)
        got_near(side_b, q)
        got_sub(q)
    rest(1)

    peak = jnp.max(top[0], axis=1, keepdims=True)
    summed = jnp.sum(total[0] * jnp.exp2(top[0] - peak), axis=1, keepdims=True)
    log_total = peak + jnp.log(summed) * LOG2E
    weighted = reward_column * ((log_total - positive) * LN2)
    labels = lax.broadcasted_iota(jnp.int32, (ROWS, 128), 1).astype(jnp.float32)
    first_sum[line] = jnp.sum(
        jnp.where(labels == policy_column, weighted, 0.0), axis=0, keepdims=True
    )
    for device in first_targets:
        pltpu.make_async_remote_copy(
            src_ref=first_sum.at[line], dst_ref=first_sum.at[line],
            send_sem=sum_sem.at[0], recv_sem=sum_sem.at[1],
            device_id=device, device_id_type=MESH,
        ).start()
    own_level = log_total - log_reward
    level[own_slot] = as_row(own_level)
    for offset, device in sorted(level_targets, key=lambda entry: -abs(entry[0])):
        pltpu.make_async_remote_copy(
            src_ref=level.at[own_slot],
            dst_ref=level.at[slot(-offset, sub)],
            send_sem=level_sem.at[LEVELS],
            recv_sem=level_sem.at[RADIUS - offset],
            device_id=device,
            device_id_type=MESH,
        ).start()
    weighted_ref[...] = as_row(weighted)

    reward_copy.wait()
    for index in range(SLOTS):
        half = index - slot(0, 0)
        value = jnp.exp2(scores[index] - own_level)
        if 0 <= half < SUBS:
            match = column_float + float(half * ROWS) == partner_column
            value = value - jnp.where(match, reward_column + rewards[half], 0.0)
        shares[index] = value

    def await_rows(ref, count, sem):
        part = ref.at[pl.ds(0, count)]
        pltpu.make_async_copy(part, part, sem).wait()

    await_rows(first_sum, GROUP - 1, sum_sem.at[1])
    second_sum[plane] = jnp.sum(first_sum[...], axis=0)
    for device in second_targets:
        pltpu.make_async_remote_copy(
            src_ref=second_sum.at[plane], dst_ref=second_sum.at[plane],
            send_sem=sum_sem.at[2], recv_sem=sum_sem.at[3],
            device_id=device, device_id_type=MESH,
        ).start()
    toward_a = 2 * side_a - 1
    offsets = [0] + [toward_a * k for k in range(1, RADIUS + 1)]
    offsets += [-toward_a * k for k in range(1, RADIUS + 1)]
    for begin in range(0, LEVELS, SPAN):
        group = offsets[begin : begin + SPAN]
        for number, offset in enumerate(group):
            await_rows(level, SUBS - (begin + number == 0), level_sem.at[RADIUS + offset])
        product = None
        for offset in group:
            values = []
            for half in range(SUBS):
                index = slot(offset, half)
                value = shares[index] + jnp.exp2(scores[index] - level[index])
                values.append(value.astype(jnp.bfloat16))
            term = jnp.dot(
                jnp.concatenate(values, axis=1),
                keys[pl.ds(pl.multiple_of(slot(offset, 0) * ROWS, BLOCK), BLOCK), :],
                preferred_element_type=jnp.float32,
            )
            product = term if product is None else product + term
        gradient_ref[...] = product if begin == 0 else gradient_ref[...] + product

    await_rows(second_sum, GROUP - 1, sum_sem.at[3])
    loss = jnp.sum(second_sum[...], axis=0) * (POLICIES / (LOOP * BLOCK))
    loss_ref[...] = loss[:, :POLICIES]

    await_rows(level, SLOTS - 1, level_sem.at[LEVELS])
    await_rows(first_sum, GROUP - 1, sum_sem.at[0])
    await_rows(second_sum, GROUP - 1, sum_sem.at[2])
    def await_sent(link, count):
        part = keys.at[pl.ds(0, count)]
        pltpu.make_async_copy(part, part, send.at[link]).wait()

    moved = MOVED * PART
    await_sent(side_a, 3 * ROWS)
    await_sent(side_b, 3 * ROWS - moved)
    await_sent(SUB, 3 * ROWS)
    await_sent(CORE, 8 * ROWS)

    @pl.when(z != 0)
    def _():
        await_sent(side_b, moved)

    @pl.when(z == LINE - 1)
    def _():
        await_sent(SUB, moved)


def finish(a_ref, b_ref, c_ref, a_out, b_out, c_out, sems):
    step = ROWS // PIECES
    pairs = [(b_ref.at[r], b_out.at[r]) for r in (pl.ds(i * step, step) for i in range(PIECES))]
    pairs += [(a_ref, a_out), (c_ref, c_out)]
    copies = [pltpu.make_async_copy(p, q, sems.at[i]) for i, (p, q) in enumerate(pairs)]
    for copy in copies:
        copy.start()
    for copy in copies:
        copy.wait()


def body(embeddings, reward, partner, policy):
    vmem = pl.BlockSpec(memory_space=pltpu.VMEM)
    hbm = pl.BlockSpec(memory_space=pltpu.HBM)
    outs = (
        jax.ShapeDtypeStruct((1, ROWS), jnp.float32),
        jax.ShapeDtypeStruct((ROWS, WIDTH), jnp.float32),
        jax.ShapeDtypeStruct((1, POLICIES), jnp.float32),
    )
    results = pl.pallas_call(
        kernel,
        out_shape=outs,
        in_specs=[hbm, hbm, hbm, hbm],
        out_specs=(vmem, vmem, vmem),
        scratch_shapes=[
            pltpu.VMEM((SLOTS * ROWS, WIDTH), jnp.bfloat16),
            pltpu.VMEM((SLOTS, ROWS, ROWS), jnp.float32),
            pltpu.VMEM((SLOTS, ROWS, ROWS), jnp.float32),
            pltpu.VMEM((SLOTS, 1, ROWS), jnp.float32),
            pltpu.VMEM((SUBS, 1, ROWS), jnp.float32),
            pltpu.VMEM((2, 1, ROWS), jnp.int32),
            pltpu.VMEM((GROUP, 1, 128), jnp.float32),
            pltpu.VMEM((GROUP, 1, 128), jnp.float32),
            pltpu.SemaphoreType.DMA((CLASSES, CHUNKS)),
            pltpu.SemaphoreType.DMA((4,)),
            pltpu.SemaphoreType.DMA((LEVELS + 1,)),
            pltpu.SemaphoreType.DMA((4,)),
            pltpu.SemaphoreType.DMA((2,)),
            pltpu.SemaphoreType.DMA((4,)),
        ],
        name="band",
        compiler_params=pltpu.CompilerParams(
            collective_id=0, has_side_effects=True, vmem_limit_bytes=48 * 2**20
        ),
    )(
        *(
            pltpu.with_memory_space_constraint(a, pltpu.HBM)
            for a in (
                embeddings, reward.reshape(1, ROWS), partner.reshape(1, ROWS), policy.reshape(1, ROWS)
            )
        )
    )
    weighted, gradient, loss = pl.pallas_call(
        finish,
        out_shape=outs,
        in_specs=[vmem, vmem, vmem],
        out_specs=(hbm, hbm, hbm),
        scratch_shapes=[pltpu.SemaphoreType.DMA((PIECES + 2,))],
        name="finish",
        compiler_params=pltpu.CompilerParams(vmem_limit_bytes=8 * 2**20),
    )(*results)
    return weighted.reshape(ROWS), gradient, loss.reshape(POLICIES)


def solution(mesh):
    rows = P(("loop", "sub"))
    matrix = P(("loop", "sub"), None)
    return jax.shard_map(
        body, mesh=mesh, in_specs=(matrix, rows, rows, rows),
        out_specs=(rows, matrix, P()), check_vma=False,
    )
```

```python
import functools
import math

import jax
import jax.numpy as jnp
from jax import lax
from jax.experimental import pallas as pl
from jax.experimental.pallas import tpu as pltpu
from jax.sharding import PartitionSpec as P

RADIUS = 4
POLICIES = 16
ROWS = 256
WIDTH = 1024
SUBS = 2
BLOCK = ROWS * SUBS
LOOP = 128
SEAM = 64
CHUNKS = 8
LINE = 8
MOVED = 2
SPAN = 3
LEVELS = 2 * RADIUS + 1
TURNS = 4
PIECES = 4
PART = ROWS // CHUNKS
SLOTS = (2 * RADIUS + 1) * SUBS
GROUP = 16
LOG2E = 1.4426950408889634
LN2 = 0.6931471805599453
LOWEST = -1e30
MESH = pl.DeviceIdType.MESH

OWN, HALF, FAR, SUB_FAR = 0, 2, 4, 6
CORE_NEAR_A, CORE_NEAR_B = 8, 10
SUB_OWN, CORE_OWN, CORE_HALF, CORE_FAR_A, CORE_FAR_B = 12, 13, 14, 15, 16
CLASSES = 17


def slot(offset, half):
    return (offset + RADIUS) * SUBS + half


def kernel(
    x_ref, reward_ref, partner_ref, policy_ref,
    weighted_ref, gradient_ref, loss_ref,
    keys, scores, shares, level, rewards, integers, first_sum, second_sum,
    recv, send, level_sem, sum_sem, reward_sem, local_sem, word_sem,
):
    block = lax.axis_index("loop")
    sub = lax.axis_index("sub")
    core = lax.rem(block, 2)

    def crosses(at):
        return jnp.where(lax.rem(at, SEAM) >= SEAM - 2, 1, 0)

    def flip(half, by):
        return half + by - 2 * half * by

    def at_loop(index):
        return lax.rem(index + LOOP, LOOP)

    cross_up = crosses(block)
    cross_low = crosses(at_loop(block - 2))
    cross_up2 = crosses(at_loop(block + 2))
    cross_low2 = crosses(at_loop(block - 4))
    up_dev = (at_loop(block + 2), flip(sub, cross_up))
    low_dev = (at_loop(block - 2), flip(sub, cross_low))
    sub_dev = (block, 1 - sub)
    core_dev = (block + 1 - 2 * core, sub)
    low_half = flip(sub, cross_low)
    up_half = flip(sub, cross_up)
    low_far = flip(low_half, cross_low2)
    up_far = flip(up_half, cross_up2)

    own_slot = slot(0, sub)
    half_slot = slot(0, 1 - sub)

    def piece(index):
        return pl.ds(pl.multiple_of(index * ROWS, ROWS), ROWS)

    loads = [
        pltpu.make_async_copy(x_ref, keys.at[piece(own_slot)], local_sem.at[0]),
        pltpu.make_async_copy(reward_ref, rewards.at[sub], local_sem.at[1]),
        pltpu.make_async_copy(partner_ref, integers.at[0], local_sem.at[2]),
        pltpu.make_async_copy(policy_ref, integers.at[1], local_sem.at[3]),
    ]
    for load in loads:
        load.start()

    level_targets = []
    for offset in sorted(range(-RADIUS, RADIUS + 1), key=lambda k: (k % 2, abs(k))):
        for other in range(SUBS):
            if offset == 0 and other == 0:
                continue
            level_targets.append((offset, (at_loop(block + offset), flip(sub, other))))
    line = lax.rem(block, GROUP)
    line_base = block - line
    farthest = sorted(range(1, GROUP), key=lambda i: -min(i, GROUP - i))
    first_targets = [(line_base + lax.rem(line + i, GROUP), sub) for i in farthest]
    plane = (block // GROUP) * SUBS + sub
    second_targets = []
    for i in farthest:
        other = lax.rem(plane + i, GROUP)
        second_targets.append(((other // SUBS) * GROUP + line, lax.rem(other, SUBS)))
    barrier = pltpu.get_barrier_semaphore()
    x_base = block - lax.rem(block, SEAM)
    beside = [
        core_dev,
        sub_dev,
        (at_loop(block + SEAM), 1 - sub),
        (line_base + lax.rem(line + 2, GROUP), sub),
        (line_base + lax.rem(line + GROUP - 2, GROUP), sub),
        (x_base + lax.rem(block + GROUP, SEAM), sub),
        (x_base + lax.rem(block + SEAM - GROUP, SEAM), sub),
    ]
    greeted = [low_dev, up_dev] + beside
    for device in greeted:
        pl.semaphore_signal(barrier, inc=1, device_id=device, device_id_type=MESH)
    for load in loads:
        load.wait()
    pl.semaphore_wait(barrier, len(greeted))

    def tell(turn):
        for device in beside:
            pl.semaphore_signal(
                word_sem.at[turn], inc=1, device_id=device, device_id_type=MESH
            )

    def hear(turn):
        pl.semaphore_wait(word_sem.at[turn], len(beside))

    def rows(index, q):
        return pl.ds(pl.multiple_of(index * ROWS + q * PART, PART), PART)

    def push(source, target, kind, q, link, device):
        pltpu.make_async_remote_copy(
            src_ref=keys.at[rows(source, q)],
            dst_ref=keys.at[rows(target, q)],
            send_sem=send.at[link],
            recv_sem=recv.at[kind, q],
            device_id=device,
            device_id_type=MESH,
        ).start()

    def await_piece(kind, q):
        ref = keys.at[pl.ds(0, PART)]
        pltpu.make_async_copy(ref, ref, recv.at[kind, q]).wait()

    SUB, CORE = 2, 3
    shift = 2 * core - 1

    z = lax.rem(block // 2, LINE)
    side_b = jnp.where(z >= LINE // 2, 1, 0)
    side_a = 1 - side_b
    edge = jnp.where(jnp.logical_or(z < 2, z >= LINE - 2), 1, 0)

    def pick(side, low, up):
        return low + side * (up - low)

    def near(side):
        return 4 * side - 2

    def device_of(side):
        return tuple(pick(side, low, up) for low, up in zip(low_dev, up_dev))

    def near_half(side):
        return pick(side, low_half, up_half)

    def far_half_of(side):
        return pick(side, low_far, up_far)

    def to_core(offset, half, kind, q):
        push(slot(offset, half), slot(offset + shift, half), kind, q, CORE, core_dev)

    def send_own(side, *chunks):
        for q in chunks:
            push(own_slot, slot(-near(side), sub), OWN + 1 - side, q, side, device_of(side))

    def send_half(side, *chunks):
        for q in chunks:
            push(
                half_slot, slot(-near(side), 1 - sub), HALF + 1 - side, q, side,
                device_of(side),
            )

    def got_own(side, q):
        other = 1 - side
        await_piece(OWN + side, q)
        half = near_half(side)
        push(
            slot(near(side), half), slot(-2 * near(other), half), FAR + side, q, other,
            device_of(other),
        )

    def spread_own(side, q):
        to_core(near(side), near_half(side), CORE_NEAR_A + side, q)

    def got_half(q):
        await_piece(SUB_OWN, q)
        to_core(0, 1 - sub, CORE_HALF, q)

    far_offset = 4 - 8 * core
    far_half = far_half_of(1 - core)

    def got_far(side, q):
        await_piece(FAR + side, q)
        at = slot(2 * near(side), far_half_of(side))
        push(at, at, SUB_FAR + side, q, SUB, sub_dev)

    def spread_far(q):
        to_core(far_offset, far_half, CORE_FAR_A, q)

    def got_near(side, q):
        await_piece(HALF + side, q)
        to_core(near(side), 1 - near_half(side), CORE_NEAR_B + side, q)

    def got_sub(q):
        await_piece(SUB_FAR, q)
        await_piece(SUB_FAR + 1, q)
        to_core(far_offset, 1 - far_half, CORE_FAR_B, q)

    def await_all(kind):
        for q in range(CHUNKS):
            await_piece(kind, q)

    row_at = lax.broadcasted_iota(jnp.int32, (ROWS, ROWS), 0)
    column_at = lax.broadcasted_iota(jnp.int32, (ROWS, ROWS), 1)
    diagonal = row_at == column_at
    column_float = column_at.astype(jnp.float32)

    def as_column(row):
        return jnp.sum(jnp.where(diagonal, row, 0.0), axis=1, keepdims=True)

    def as_row(column):
        return jnp.sum(jnp.where(diagonal, column, 0.0), axis=0, keepdims=True)

    factor = LOG2E / math.sqrt(WIDTH)

    top = [None]
    total = [None]

    def absorb(index, part=None, own=False):
        absorb_all([index], part, own)

    def absorb_all(indices, part=None, own=False):
        first, count = (0, ROWS) if part is None else (part * 128, 128)
        parts = []
        for index in indices:
            block_rows = pl.ds(pl.multiple_of(index * ROWS + first, 128), count)
            tile = lax.dot_general(
                keys[piece(own_slot), :], keys[block_rows, :], (((1,), (1,)), ((), ())),
                preferred_element_type=jnp.float32,
            ) * factor
            if own:
                tile = jnp.where(diagonal, LOWEST, tile)
            scores[index, :, first : first + count] = tile
            parts += [tile[:, i : i + 128] for i in range(0, count, 128)]
        high = functools.reduce(jnp.maximum, parts)
        if top[0] is not None:
            high = jnp.maximum(high, top[0])
        fresh = functools.reduce(jnp.add, [jnp.exp2(t - high) for t in parts])
        if top[0] is not None:
            fresh = fresh + total[0] * jnp.exp2(top[0] - high)
        top[0], total[0] = high, fresh

    for q in range(4):
        send_own(side_a, q)
        send_own(side_b, q)
        push(own_slot, own_slot, SUB_OWN, q, SUB, sub_dev)

    @pl.when(edge == 1)
    def _():
        send_own(side_a, 4, 5)

    for q in range(4, CHUNKS):
        push(own_slot, own_slot, SUB_OWN, q, SUB, sub_dev)

    def near_a(q):
        got_own(side_a, q)
        if q < 4:
            send_own(side_b, q + 4)
        elif q < 7:
            send_half(side_b, q - 4)
        else:
            send_half(side_b, *range(3, CHUNKS - MOVED))

            @pl.when(z != 0)
            def _():
                send_half(side_b, *range(CHUNKS - MOVED, CHUNKS))
        spread_own(side_a, q)

    def near_b(q):
        got_own(side_b, q)
        if q < 2:
            send_own(side_a, q + 4 + 2 * edge)
        elif q < 4:

            @pl.when(edge == 1)
            def _():
                send_half(side_a, q - 2)

            @pl.when(edge == 0)
            def _():
                send_own(side_a, q + 4)
        else:
            send_half(side_a, q - 4 + 2 * edge)
        if q == 7:

            @pl.when(edge == 0)
            def _():
                send_half(side_a, 4, 5)

            send_half(side_a, 6, 7)
        if q >= CHUNKS - MOVED:
            at = slot(near(side_b), near_half(side_b))

            @pl.when(z == LINE - 1)
            def _():
                push(at, at, HALF + side_b, q, SUB, sub_dev)
        spread_own(side_b, q)

    def far_a(q):
        got_far(side_a, q)

    def far_b(q):
        got_far(side_b, q)
        spread_far(q)

    near_a(0)
    for q in range(CHUNKS):
        push(own_slot, slot(shift, sub), CORE_OWN, q, CORE, core_dev)
    reward_copy = pltpu.make_async_remote_copy(
        src_ref=rewards.at[sub], dst_ref=rewards.at[sub],
        send_sem=reward_sem.at[0], recv_sem=reward_sem.at[1],
        device_id=sub_dev, device_id_type=MESH,
    )
    reward_copy.start()
    near_a(1)
    tell(0)
    absorb(own_slot, own=True)
    near_a(2)
    near_b(0)
    near_a(3)
    near_b(1)
    far_a(0)
    for q in range(3):
        got_half(q)
    near_b(2)
    near_a(4)
    near_b(3)
    far_a(1)
    hear(0)
    tell(1)
    await_all(CORE_OWN)
    absorb(slot(-shift, sub))
    near_a(5)
    far_b(0)
    far_a(2)
    for q in range(3, CHUNKS):
        got_half(q)
    near_b(4)
    near_a(6)
    far_b(1)
    near_b(5)
    far_a(3)
    absorb(half_slot)
    near_a(7)
    far_b(2)
    hear(1)
    tell(2)
    near_b(6)
    far_a(4)
    reward_row = rewards[sub]
    reward_column = as_column(reward_row)
    partner_column = as_column((integers[0] - block * BLOCK).astype(jnp.float32))
    policy_column = as_column(integers[1].astype(jnp.float32))
    log_reward = jnp.log(reward_column) * LOG2E
    absorb(slot(near(side_a), near_half(side_a)))
    far_b(3)
    near_b(7)
    far_a(5)
    await_all(CORE_HALF)
    absorb(slot(-shift, 1 - sub))
    absorb(slot(near(side_b), near_half(side_b)))
    far_b(4)
    hear(2)
    tell(3)
    await_all(CORE_NEAR_A + side_a)
    absorb(slot(near(side_a) - shift, near_half(side_a)))
    far_a(6)
    await_all(CORE_NEAR_A + side_b)
    absorb(slot(near(side_b) - shift, near_half(side_b)))
    own_match = column_float + (sub * ROWS).astype(jnp.float32) == partner_column
    half_match = column_float + ((1 - sub) * ROWS).astype(jnp.float32) == partner_column
    positive = jnp.sum(
        jnp.where(own_match, scores[own_slot], 0.0)
        + jnp.where(half_match, scores[half_slot], 0.0),
        axis=1, keepdims=True,
    )
    far_b(5)
    absorb(slot(2 * near(side_a), far_half_of(side_a)), 0)
    far_a(7)
    absorb(slot(2 * near(side_b), far_half_of(side_b)), 0)
    for q in range(3):
        got_sub(q)
        got_near(side_a, q)
        got_near(side_b, q)
    far_b(6)
    hear(3)
    absorb(slot(2 * near(side_a), far_half_of(side_a)), 1)
    core_far = -far_offset - shift
    core_far_half = far_half_of(core)
    got_sub(3)
    got_near(side_a, 3)
    got_near(side_b, 3)
    far_b(7)

    def await_some(kind, part):
        for q in range(part * CHUNKS // 2, (part + 1) * CHUNKS // 2):
            await_piece(kind, q)

    def rest(part):
        sides = (side_a, side_b)
        absorb_all(
            [slot(near(side), 1 - near_half(side)) for side in sides]
            + [slot(2 * near(side), 1 - far_half_of(side)) for side in sides],
            part,
        )
        for side in sides:
            await_some(CORE_NEAR_B + side, part)
        await_some(CORE_FAR_B, part)
        absorb_all(
            [slot(near(side) - shift, 1 - near_half(side)) for side in sides]
            + [slot(core_far, 1 - core_far_half)],
            part,
        )

    rest(0)
    absorb(slot(2 * near(side_b), far_half_of(side_b)), 1)
    await_all(CORE_FAR_A)
    absorb(slot(core_far, core_far_half))
    for q in range(4, CHUNKS):
        got_near(side_a, q)
        got_near(side_b, q)
        got_sub(q)
    rest(1)

    peak = jnp.max(top[0], axis=1, keepdims=True)
    summed = jnp.sum(total[0] * jnp.exp2(top[0] - peak), axis=1, keepdims=True)
    log_total = peak + jnp.log(summed) * LOG2E
    weighted = reward_column * ((log_total - positive) * LN2)
    labels = lax.broadcasted_iota(jnp.int32, (ROWS, 128), 1).astype(jnp.float32)
    first_sum[line] = jnp.sum(
        jnp.where(labels == policy_column, weighted, 0.0), axis=0, keepdims=True
    )
    for device in first_targets:
        pltpu.make_async_remote_copy(
            src_ref=first_sum.at[line], dst_ref=first_sum.at[line],
            send_sem=sum_sem.at[0], recv_sem=sum_sem.at[1],
            device_id=device, device_id_type=MESH,
        ).start()
    own_level = log_total - log_reward
    level[own_slot] = as_row(own_level)
    for offset, device in sorted(level_targets, key=lambda entry: -abs(entry[0])):
        pltpu.make_async_remote_copy(
            src_ref=level.at[own_slot],
            dst_ref=level.at[slot(-offset, sub)],
            send_sem=level_sem.at[LEVELS],
            recv_sem=level_sem.at[RADIUS - offset],
            device_id=device,
            device_id_type=MESH,
        ).start()
    weighted_ref[...] = as_row(weighted)

    reward_copy.wait()
    for index in range(SLOTS):
        half = index - slot(0, 0)
        value = jnp.exp2(scores[index] - own_level)
        if 0 <= half < SUBS:
            match = column_float + float(half * ROWS) == partner_column
            value = value - jnp.where(match, reward_column + rewards[half], 0.0)
        shares[index] = value

    def await_rows(ref, count, sem):
        part = ref.at[pl.ds(0, count)]
        pltpu.make_async_copy(part, part, sem).wait()

    await_rows(first_sum, GROUP - 1, sum_sem.at[1])
    second_sum[plane] = jnp.sum(first_sum[...], axis=0)
    for device in second_targets:
        pltpu.make_async_remote_copy(
            src_ref=second_sum.at[plane], dst_ref=second_sum.at[plane],
            send_sem=sum_sem.at[2], recv_sem=sum_sem.at[3],
            device_id=device, device_id_type=MESH,
        ).start()
    toward_a = 2 * side_a - 1
    offsets = [0] + [toward_a * k for k in range(1, RADIUS + 1)]
    offsets += [-toward_a * k for k in range(1, RADIUS + 1)]
    for begin in range(0, LEVELS, SPAN):
        group = offsets[begin : begin + SPAN]
        for number, offset in enumerate(group):
            await_rows(level, SUBS - (begin + number == 0), level_sem.at[RADIUS + offset])
        product = None
        for offset in group:
            values = []
            for half in range(SUBS):
                index = slot(offset, half)
                value = shares[index] + jnp.exp2(scores[index] - level[index])
                values.append(value.astype(jnp.bfloat16))
            term = jnp.dot(
                jnp.concatenate(values, axis=1),
                keys[pl.ds(pl.multiple_of(slot(offset, 0) * ROWS, BLOCK), BLOCK), :],
                preferred_element_type=jnp.float32,
            )
            product = term if product is None else product + term
        gradient_ref[...] = product if begin == 0 else gradient_ref[...] + product

    await_rows(second_sum, GROUP - 1, sum_sem.at[3])
    loss = jnp.sum(second_sum[...], axis=0) * (POLICIES / (LOOP * BLOCK))
    loss_ref[...] = loss[:, :POLICIES]

    await_rows(level, SLOTS - 1, level_sem.at[LEVELS])
    await_rows(first_sum, GROUP - 1, sum_sem.at[0])
    await_rows(second_sum, GROUP - 1, sum_sem.at[2])
    def await_sent(link, count):
        part = keys.at[pl.ds(0, count)]
        pltpu.make_async_copy(part, part, send.at[link]).wait()

    moved = MOVED * PART
    await_sent(side_a, 3 * ROWS)
    await_sent(side_b, 3 * ROWS - moved)
    await_sent(SUB, 3 * ROWS)
    await_sent(CORE, 8 * ROWS)

    @pl.when(z != 0)
    def _():
        await_sent(side_b, moved)

    @pl.when(z == LINE - 1)
    def _():
        await_sent(SUB, moved)


def finish(a_ref, b_ref, c_ref, a_out, b_out, c_out, sems):
    step = ROWS // PIECES
    pairs = [(b_ref.at[r], b_out.at[r]) for r in (pl.ds(i * step, step) for i in range(PIECES))]
    pairs += [(a_ref, a_out), (c_ref, c_out)]
    copies = [pltpu.make_async_copy(p, q, sems.at[i]) for i, (p, q) in enumerate(pairs)]
    for copy in copies:
        copy.start()
    for copy in copies:
        copy.wait()


def body(embeddings, reward, partner, policy):
    vmem = pl.BlockSpec(memory_space=pltpu.VMEM)
    hbm = pl.BlockSpec(memory_space=pltpu.HBM)
    outs = (
        jax.ShapeDtypeStruct((1, ROWS), jnp.float32),
        jax.ShapeDtypeStruct((ROWS, WIDTH), jnp.float32),
        jax.ShapeDtypeStruct((1, POLICIES), jnp.float32),
    )
    results = pl.pallas_call(
        kernel,
        out_shape=outs,
        in_specs=[hbm, hbm, hbm, hbm],
        out_specs=(vmem, vmem, vmem),
        scratch_shapes=[
            pltpu.VMEM((SLOTS * ROWS, WIDTH), jnp.bfloat16),
            pltpu.VMEM((SLOTS, ROWS, ROWS), jnp.float32),
            pltpu.VMEM((SLOTS, ROWS, ROWS), jnp.float32),
            pltpu.VMEM((SLOTS, 1, ROWS), jnp.float32),
            pltpu.VMEM((SUBS, 1, ROWS), jnp.float32),
            pltpu.VMEM((2, 1, ROWS), jnp.int32),
            pltpu.VMEM((GROUP, 1, 128), jnp.float32),
            pltpu.VMEM((GROUP, 1, 128), jnp.float32),
            pltpu.SemaphoreType.DMA((CLASSES, CHUNKS)),
            pltpu.SemaphoreType.DMA((4,)),
            pltpu.SemaphoreType.DMA((LEVELS + 1,)),
            pltpu.SemaphoreType.DMA((4,)),
            pltpu.SemaphoreType.DMA((2,)),
            pltpu.SemaphoreType.DMA((4,)),
            pltpu.SemaphoreType.REGULAR((TURNS,)),
        ],
        name="band",
        compiler_params=pltpu.CompilerParams(
            collective_id=0, has_side_effects=True, vmem_limit_bytes=48 * 2**20
        ),
    )(
        *(
            pltpu.with_memory_space_constraint(a, pltpu.HBM)
            for a in (
                embeddings, reward.reshape(1, ROWS), partner.reshape(1, ROWS), policy.reshape(1, ROWS)
            )
        )
    )
    weighted, gradient, loss = pl.pallas_call(
        finish,
        out_shape=outs,
        in_specs=[vmem, vmem, vmem],
        out_specs=(hbm, hbm, hbm),
        scratch_shapes=[pltpu.SemaphoreType.DMA((PIECES + 2,))],
        name="finish",
        compiler_params=pltpu.CompilerParams(vmem_limit_bytes=8 * 2**20),
    )(*results)
    return weighted.reshape(ROWS), gradient, loss.reshape(POLICIES)


def solution(mesh):
    rows = P(("loop", "sub"))
    matrix = P(("loop", "sub"), None)
    return jax.shard_map(
        body, mesh=mesh, in_specs=(matrix, rows, rows, rows),
        out_specs=(rows, matrix, P()), check_vma=False,
    )
```

```python
import functools
import math

import jax
import jax.numpy as jnp
from jax import lax
from jax.experimental import pallas as pl
from jax.experimental.pallas import tpu as pltpu
from jax.sharding import PartitionSpec as P

RADIUS = 4
POLICIES = 16
ROWS = 256
WIDTH = 1024
SUBS = 2
BLOCK = ROWS * SUBS
LOOP = 128
SEAM = 64
CHUNKS = 8
LINE = 8
MOVED = 2
LEVELS = 2 * RADIUS + 1
TURNS = 4
PIECES = 4
PART = ROWS // CHUNKS
SLOTS = (2 * RADIUS + 1) * SUBS
GROUP = 16
LOG2E = 1.4426950408889634
LN2 = 0.6931471805599453
LOWEST = -1e30
MESH = pl.DeviceIdType.MESH

OWN, HALF, FAR, SUB_FAR = 0, 2, 4, 6
CORE_NEAR_A, CORE_NEAR_B = 8, 10
SUB_OWN, CORE_OWN, CORE_HALF, CORE_FAR_A, CORE_FAR_B = 12, 13, 14, 15, 16
CLASSES = 17


def slot(offset, half):
    return (offset + RADIUS) * SUBS + half


def kernel(
    x_ref, reward_ref, partner_ref, policy_ref,
    weighted_ref, gradient_ref, loss_ref,
    keys, scores, level, rewards, integers, first_sum, second_sum,
    recv, send, level_sem, sum_sem, reward_sem, local_sem, word_sem,
):
    block = lax.axis_index("loop")
    sub = lax.axis_index("sub")
    core = lax.rem(block, 2)

    def crosses(at):
        return jnp.where(lax.rem(at, SEAM) >= SEAM - 2, 1, 0)

    def flip(half, by):
        return half + by - 2 * half * by

    def at_loop(index):
        return lax.rem(index + LOOP, LOOP)

    cross_up = crosses(block)
    cross_low = crosses(at_loop(block - 2))
    cross_up2 = crosses(at_loop(block + 2))
    cross_low2 = crosses(at_loop(block - 4))
    up_dev = (at_loop(block + 2), flip(sub, cross_up))
    low_dev = (at_loop(block - 2), flip(sub, cross_low))
    sub_dev = (block, 1 - sub)
    core_dev = (block + 1 - 2 * core, sub)
    low_half = flip(sub, cross_low)
    up_half = flip(sub, cross_up)
    low_far = flip(low_half, cross_low2)
    up_far = flip(up_half, cross_up2)

    own_slot = slot(0, sub)
    half_slot = slot(0, 1 - sub)

    def piece(index):
        return pl.ds(pl.multiple_of(index * ROWS, ROWS), ROWS)

    loads = [
        pltpu.make_async_copy(x_ref, keys.at[piece(own_slot)], local_sem.at[0]),
        pltpu.make_async_copy(reward_ref, rewards.at[sub], local_sem.at[1]),
        pltpu.make_async_copy(partner_ref, integers.at[0], local_sem.at[2]),
        pltpu.make_async_copy(policy_ref, integers.at[1], local_sem.at[3]),
    ]
    for load in loads:
        load.start()

    line = lax.rem(block, GROUP)
    line_base = block - line
    first_targets = [(line_base + lax.rem(line + i, GROUP), sub) for i in range(1, GROUP)]
    plane = (block // GROUP) * SUBS + sub
    x = lax.rem(block // GROUP, 4)
    y = (block // SEAM) * SUBS + sub
    steps = [(dx, dy) for dx in range(4) for dy in range(4) if dx or dy]
    steps.sort(key=lambda step: sum(min(d, 4 - d) for d in step))
    second_targets = []
    for dx, dy in steps:
        at_x, at_y = lax.rem(x + dx, 4), lax.rem(y + dy, 4)
        second_targets.append(
            ((at_y // SUBS) * SEAM + at_x * GROUP + line, lax.rem(at_y, SUBS))
        )
    barrier = pltpu.get_barrier_semaphore()
    x_base = block - lax.rem(block, SEAM)
    beside = [
        core_dev,
        sub_dev,
        (at_loop(block + SEAM), 1 - sub),
        (line_base + lax.rem(line + 2, GROUP), sub),
        (line_base + lax.rem(line + GROUP - 2, GROUP), sub),
        (x_base + lax.rem(block + GROUP, SEAM), sub),
        (x_base + lax.rem(block + SEAM - GROUP, SEAM), sub),
    ]
    greeted = [low_dev, up_dev] + beside
    for device in greeted:
        pl.semaphore_signal(barrier, inc=1, device_id=device, device_id_type=MESH)
    for load in loads:
        load.wait()
    pl.semaphore_wait(barrier, len(greeted))

    def tell(turn):
        for device in beside:
            pl.semaphore_signal(
                word_sem.at[turn], inc=1, device_id=device, device_id_type=MESH
            )

    def hear(turn):
        pl.semaphore_wait(word_sem.at[turn], len(beside))

    def rows(index, q):
        return pl.ds(pl.multiple_of(index * ROWS + q * PART, PART), PART)

    def push(source, target, kind, q, link, device):
        pltpu.make_async_remote_copy(
            src_ref=keys.at[rows(source, q)],
            dst_ref=keys.at[rows(target, q)],
            send_sem=send.at[link],
            recv_sem=recv.at[kind, q],
            device_id=device,
            device_id_type=MESH,
        ).start()

    def await_piece(kind, q):
        ref = keys.at[pl.ds(0, PART)]
        pltpu.make_async_copy(ref, ref, recv.at[kind, q]).wait()

    SUB, CORE = 2, 3
    shift = 2 * core - 1

    z = lax.rem(block // 2, LINE)
    side_b = jnp.where(z >= LINE // 2, 1, 0)
    side_a = 1 - side_b
    edge = jnp.where(jnp.logical_or(z < 2, z >= LINE - 2), 1, 0)

    def pick(side, low, up):
        return low + side * (up - low)

    def near(side):
        return 4 * side - 2

    def device_of(side):
        return tuple(pick(side, low, up) for low, up in zip(low_dev, up_dev))

    def near_half(side):
        return pick(side, low_half, up_half)

    def far_half_of(side):
        return pick(side, low_far, up_far)

    def to_core(offset, half, kind, q):
        push(slot(offset, half), slot(offset + shift, half), kind, q, CORE, core_dev)

    def send_own(side, *chunks):
        for q in chunks:
            push(own_slot, slot(-near(side), sub), OWN + 1 - side, q, side, device_of(side))

    def send_half(side, *chunks):
        for q in chunks:
            push(
                half_slot, slot(-near(side), 1 - sub), HALF + 1 - side, q, side,
                device_of(side),
            )

    def got_own(side, q):
        other = 1 - side
        await_piece(OWN + side, q)
        half = near_half(side)
        push(
            slot(near(side), half), slot(-2 * near(other), half), FAR + side, q, other,
            device_of(other),
        )

    def spread_own(side, q):
        to_core(near(side), near_half(side), CORE_NEAR_A + side, q)

    def got_half(q):
        await_piece(SUB_OWN, q)
        to_core(0, 1 - sub, CORE_HALF, q)

    far_offset = 4 - 8 * core
    far_half = far_half_of(1 - core)

    def got_far(side, q):
        await_piece(FAR + side, q)
        at = slot(2 * near(side), far_half_of(side))
        push(at, at, SUB_FAR + side, q, SUB, sub_dev)

    def spread_far(q):
        to_core(far_offset, far_half, CORE_FAR_A, q)

    def got_near(side, q):
        await_piece(HALF + side, q)
        to_core(near(side), 1 - near_half(side), CORE_NEAR_B + side, q)

    def got_sub(q):
        await_piece(SUB_FAR, q)
        await_piece(SUB_FAR + 1, q)
        to_core(far_offset, 1 - far_half, CORE_FAR_B, q)

    def await_all(kind):
        for q in range(CHUNKS):
            await_piece(kind, q)

    row_at = lax.broadcasted_iota(jnp.int32, (ROWS, ROWS), 0)
    column_at = lax.broadcasted_iota(jnp.int32, (ROWS, ROWS), 1)
    diagonal = row_at == column_at
    column_float = column_at.astype(jnp.float32)

    def as_column(row):
        return jnp.sum(jnp.where(diagonal, row, 0.0), axis=1, keepdims=True)

    def as_row(column):
        return jnp.sum(jnp.where(diagonal, column, 0.0), axis=0, keepdims=True)

    factor = LOG2E / math.sqrt(WIDTH)

    top = [None]
    total = [None]

    def absorb(index, part=None, own=False):
        absorb_all([index], part, own)

    def absorb_all(indices, part=None, own=False):
        first, count = (0, ROWS) if part is None else (part * 128, 128)
        parts = []
        for index in indices:
            block_rows = pl.ds(pl.multiple_of(index * ROWS + first, 128), count)
            tile = lax.dot_general(
                keys[piece(own_slot), :], keys[block_rows, :], (((1,), (1,)), ((), ())),
                preferred_element_type=jnp.float32,
            ) * factor
            if own:
                tile = jnp.where(diagonal, LOWEST, tile)
            scores[index, :, first : first + count] = tile
            parts += [tile[:, i : i + 128] for i in range(0, count, 128)]
        high = functools.reduce(jnp.maximum, parts)
        if top[0] is not None:
            high = jnp.maximum(high, top[0])
        fresh = functools.reduce(jnp.add, [jnp.exp2(t - high) for t in parts])
        if top[0] is not None:
            fresh = fresh + total[0] * jnp.exp2(top[0] - high)
        top[0], total[0] = high, fresh

    for q in range(4):
        send_own(side_a, q)
        send_own(side_b, q)
        push(own_slot, own_slot, SUB_OWN, q, SUB, sub_dev)

    @pl.when(edge == 1)
    def _():
        send_own(side_a, 4, 5)

    for q in range(4, CHUNKS):
        push(own_slot, own_slot, SUB_OWN, q, SUB, sub_dev)

    def near_a(q):
        got_own(side_a, q)
        if q < 4:
            send_own(side_b, q + 4)
        elif q < 7:
            send_half(side_b, q - 4)
        else:
            send_half(side_b, *range(3, CHUNKS - MOVED))

            @pl.when(z != 0)
            def _():
                send_half(side_b, *range(CHUNKS - MOVED, CHUNKS))
        spread_own(side_a, q)

    def near_b(q):
        got_own(side_b, q)
        if q < 2:
            send_own(side_a, q + 4 + 2 * edge)
        elif q < 4:

            @pl.when(edge == 1)
            def _():
                send_half(side_a, q - 2)

            @pl.when(edge == 0)
            def _():
                send_own(side_a, q + 4)
        else:
            send_half(side_a, q - 4 + 2 * edge)
        if q == 7:

            @pl.when(edge == 0)
            def _():
                send_half(side_a, 4, 5)

            send_half(side_a, 6, 7)
        if q >= CHUNKS - MOVED:
            at = slot(near(side_b), near_half(side_b))

            @pl.when(z == LINE - 1)
            def _():
                push(at, at, HALF + side_b, q, SUB, sub_dev)
        spread_own(side_b, q)

    def far_a(q):
        got_far(side_a, q)

    def far_b(q):
        got_far(side_b, q)
        spread_far(q)

    near_a(0)
    for q in range(CHUNKS):
        push(own_slot, slot(shift, sub), CORE_OWN, q, CORE, core_dev)
    reward_copy = pltpu.make_async_remote_copy(
        src_ref=rewards.at[sub], dst_ref=rewards.at[sub],
        send_sem=reward_sem.at[0], recv_sem=reward_sem.at[1],
        device_id=sub_dev, device_id_type=MESH,
    )
    reward_copy.start()
    near_a(1)
    tell(0)
    absorb(own_slot, own=True)
    near_a(2)
    near_b(0)
    near_a(3)
    near_b(1)
    far_a(0)
    for q in range(3):
        got_half(q)
    near_b(2)
    near_a(4)
    near_b(3)
    far_a(1)
    hear(0)
    tell(1)
    await_all(CORE_OWN)
    absorb(slot(-shift, sub))
    near_a(5)
    far_b(0)
    far_a(2)
    for q in range(3, CHUNKS):
        got_half(q)
    near_b(4)
    near_a(6)
    far_b(1)
    near_b(5)
    far_a(3)
    absorb(half_slot)
    near_a(7)
    far_b(2)
    hear(1)
    tell(2)
    near_b(6)
    far_a(4)
    reward_row = rewards[sub]
    reward_column = as_column(reward_row)
    partner_column = as_column((integers[0] - block * BLOCK).astype(jnp.float32))
    policy_column = as_column(integers[1].astype(jnp.float32))
    log_reward = jnp.log(reward_column) * LOG2E
    absorb(slot(near(side_a), near_half(side_a)))
    far_b(3)
    near_b(7)
    far_a(5)
    await_all(CORE_HALF)
    absorb(slot(-shift, 1 - sub))
    absorb(slot(near(side_b), near_half(side_b)))
    far_b(4)
    hear(2)
    tell(3)
    await_all(CORE_NEAR_A + side_a)
    absorb(slot(near(side_a) - shift, near_half(side_a)))
    far_a(6)
    await_all(CORE_NEAR_A + side_b)
    absorb(slot(near(side_b) - shift, near_half(side_b)))
    own_match = column_float + (sub * ROWS).astype(jnp.float32) == partner_column
    half_match = column_float + ((1 - sub) * ROWS).astype(jnp.float32) == partner_column
    positive = jnp.sum(
        jnp.where(own_match, scores[own_slot], 0.0)
        + jnp.where(half_match, scores[half_slot], 0.0),
        axis=1, keepdims=True,
    )
    far_b(5)
    absorb(slot(2 * near(side_a), far_half_of(side_a)), 0)
    far_a(7)
    absorb(slot(2 * near(side_b), far_half_of(side_b)), 0)
    for q in range(3):
        got_sub(q)
        got_near(side_a, q)
        got_near(side_b, q)
    far_b(6)
    hear(3)
    absorb(slot(2 * near(side_a), far_half_of(side_a)), 1)
    core_far = -far_offset - shift
    core_far_half = far_half_of(core)
    got_sub(3)
    got_near(side_a, 3)
    got_near(side_b, 3)
    far_b(7)

    def await_some(kind, part):
        for q in range(part * CHUNKS // 2, (part + 1) * CHUNKS // 2):
            await_piece(kind, q)

    def rest(part):
        sides = (side_a, side_b)
        absorb_all(
            [slot(near(side), 1 - near_half(side)) for side in sides]
            + [slot(2 * near(side), 1 - far_half_of(side)) for side in sides],
            part,
        )
        for side in sides:
            await_some(CORE_NEAR_B + side, part)
        await_some(CORE_FAR_B, part)
        absorb_all(
            [slot(near(side) - shift, 1 - near_half(side)) for side in sides]
            + [slot(core_far, 1 - core_far_half)],
            part,
        )

    rest(0)
    absorb(slot(2 * near(side_b), far_half_of(side_b)), 1)
    await_all(CORE_FAR_A)
    absorb(slot(core_far, core_far_half))
    for q in range(4, CHUNKS):
        got_near(side_a, q)
        got_near(side_b, q)
        got_sub(q)
    rest(1)

    peak = jnp.max(top[0], axis=1, keepdims=True)
    summed = jnp.sum(total[0] * jnp.exp2(top[0] - peak), axis=1, keepdims=True)
    log_total = peak + jnp.log(summed) * LOG2E
    own_level = log_total - log_reward
    level[own_slot] = as_row(own_level)
    toward_a = 2 * side_a - 1

    def send_level(offset, other):
        pltpu.make_async_remote_copy(
            src_ref=level.at[own_slot],
            dst_ref=level.at[slot(-offset, sub)],
            send_sem=level_sem.at[LEVELS],
            recv_sem=level_sem.at[RADIUS - offset],
            device_id=(at_loop(block + offset), flip(sub, other)),
            device_id_type=MESH,
        ).start()

    for k in range(RADIUS, 0, -1):
        for other in range(SUBS):
            send_level(-toward_a * k, other)
    weighted = reward_column * ((log_total - positive) * LN2)
    labels = lax.broadcasted_iota(jnp.int32, (ROWS, 128), 1).astype(jnp.float32)
    first_sum[line] = jnp.sum(
        jnp.where(labels == policy_column, weighted, 0.0), axis=0, keepdims=True
    )
    for device in first_targets:
        pltpu.make_async_remote_copy(
            src_ref=first_sum.at[line], dst_ref=first_sum.at[line],
            send_sem=sum_sem.at[0], recv_sem=sum_sem.at[1],
            device_id=device, device_id_type=MESH,
        ).start()
    for k in range(RADIUS, 0, -1):
        for other in range(SUBS):
            send_level(toward_a * k, other)
    send_level(0, 1)
    weighted_ref[...] = as_row(weighted)

    def await_rows(ref, count, sem):
        part = ref.at[pl.ds(0, count)]
        pltpu.make_async_copy(part, part, sem).wait()

    await_rows(first_sum, GROUP - 1, sum_sem.at[1])
    second_sum[plane] = jnp.sum(first_sum[...], axis=0)
    for device in second_targets:
        pltpu.make_async_remote_copy(
            src_ref=second_sum.at[plane], dst_ref=second_sum.at[plane],
            send_sem=sum_sem.at[2], recv_sem=sum_sem.at[3],
            device_id=device, device_id_type=MESH,
        ).start()
    reward_copy.wait()
    runs = (
        (-RADIUS * side_b, RADIUS + 1),
        (-RADIUS + (2 * RADIUS - 1) * side_b, 2),
        (-2 + 3 * side_b, 2),
    )
    for number, (begin, count) in enumerate(runs):
        for place in range(count):
            offset = begin + place
            if number == 0 and place in (0, RADIUS):

                @pl.when(offset == 0)
                def _():
                    await_rows(level, SUBS - 1, level_sem.at[RADIUS])

                @pl.when(offset != 0)
                def _():
                    await_rows(level, SUBS, level_sem.at[RADIUS + offset])
            else:
                await_rows(level, SUBS, level_sem.at[RADIUS + offset])
        values = []
        for place in range(count):
            offset = begin + place
            for half in range(SUBS):
                index = slot(offset, half)
                tile = scores[index]
                value = jnp.exp2(tile - own_level) + jnp.exp2(tile - level[index])
                if number == 0 and place in (0, RADIUS):
                    start = (offset * BLOCK + half * ROWS).astype(jnp.float32)
                    match = column_float + start == partner_column
                    value = value - jnp.where(match, reward_column + rewards[half], 0.0)
                values.append(value.astype(jnp.bfloat16))
        inner = pl.ds(pl.multiple_of(slot(begin, 0) * ROWS, BLOCK), count * BLOCK)
        product = jnp.dot(
            jnp.concatenate(values, axis=1), keys[inner, :],
            preferred_element_type=jnp.float32,
        )
        gradient_ref[...] = product if number == 0 else gradient_ref[...] + product

    await_rows(second_sum, GROUP - 1, sum_sem.at[3])
    loss = jnp.sum(second_sum[...], axis=0) * (POLICIES / (LOOP * BLOCK))
    loss_ref[...] = loss[:, :POLICIES]

    await_rows(level, SLOTS - 1, level_sem.at[LEVELS])
    await_rows(first_sum, GROUP - 1, sum_sem.at[0])
    await_rows(second_sum, GROUP - 1, sum_sem.at[2])
    def await_sent(link, count):
        part = keys.at[pl.ds(0, count)]
        pltpu.make_async_copy(part, part, send.at[link]).wait()

    moved = MOVED * PART
    await_sent(side_a, 3 * ROWS)
    await_sent(side_b, 3 * ROWS - moved)
    await_sent(SUB, 3 * ROWS)
    await_sent(CORE, 8 * ROWS)

    @pl.when(z != 0)
    def _():
        await_sent(side_b, moved)

    @pl.when(z == LINE - 1)
    def _():
        await_sent(SUB, moved)


def finish(a_ref, b_ref, c_ref, a_out, b_out, c_out, sems):
    step = ROWS // PIECES
    pairs = [(b_ref.at[r], b_out.at[r]) for r in (pl.ds(i * step, step) for i in range(PIECES))]
    pairs = [(a_ref, a_out), (c_ref, c_out)] + pairs
    copies = [pltpu.make_async_copy(p, q, sems.at[i]) for i, (p, q) in enumerate(pairs)]
    for copy in copies:
        copy.start()
    for copy in copies:
        copy.wait()


def body(embeddings, reward, partner, policy):
    vmem = pl.BlockSpec(memory_space=pltpu.VMEM)
    hbm = pl.BlockSpec(memory_space=pltpu.HBM)
    outs = (
        jax.ShapeDtypeStruct((1, ROWS), jnp.float32),
        jax.ShapeDtypeStruct((ROWS, WIDTH), jnp.float32),
        jax.ShapeDtypeStruct((1, POLICIES), jnp.float32),
    )
    results = pl.pallas_call(
        kernel,
        out_shape=outs,
        in_specs=[hbm, hbm, hbm, hbm],
        out_specs=(vmem, vmem, vmem),
        scratch_shapes=[
            pltpu.VMEM((SLOTS * ROWS, WIDTH), jnp.bfloat16),
            pltpu.VMEM((SLOTS, ROWS, ROWS), jnp.float32),
            pltpu.VMEM((SLOTS, 1, ROWS), jnp.float32),
            pltpu.VMEM((SUBS, 1, ROWS), jnp.float32),
            pltpu.VMEM((2, 1, ROWS), jnp.int32),
            pltpu.VMEM((GROUP, 1, 128), jnp.float32),
            pltpu.VMEM((GROUP, 1, 128), jnp.float32),
            pltpu.SemaphoreType.DMA((CLASSES, CHUNKS)),
            pltpu.SemaphoreType.DMA((4,)),
            pltpu.SemaphoreType.DMA((LEVELS + 1,)),
            pltpu.SemaphoreType.DMA((4,)),
            pltpu.SemaphoreType.DMA((2,)),
            pltpu.SemaphoreType.DMA((4,)),
            pltpu.SemaphoreType.REGULAR((TURNS,)),
        ],
        name="band",
        compiler_params=pltpu.CompilerParams(
            collective_id=0, has_side_effects=True, vmem_limit_bytes=48 * 2**20
        ),
    )(
        *(
            pltpu.with_memory_space_constraint(a, pltpu.HBM)
            for a in (
                embeddings, reward.reshape(1, ROWS), partner.reshape(1, ROWS), policy.reshape(1, ROWS)
            )
        )
    )
    weighted, gradient, loss = pl.pallas_call(
        finish,
        out_shape=outs,
        in_specs=[vmem, vmem, vmem],
        out_specs=(hbm, hbm, hbm),
        scratch_shapes=[pltpu.SemaphoreType.DMA((PIECES + 2,))],
        name="finish",
        compiler_params=pltpu.CompilerParams(vmem_limit_bytes=8 * 2**20),
    )(*results)
    return weighted.reshape(ROWS), gradient, loss.reshape(POLICIES)


def solution(mesh):
    rows = P(("loop", "sub"))
    matrix = P(("loop", "sub"), None)
    return jax.shard_map(
        body, mesh=mesh, in_specs=(matrix, rows, rows, rows),
        out_specs=(rows, matrix, P()), check_vma=False,
    )
```

```python
import functools
import math

import jax
import jax.numpy as jnp
from jax import lax
from jax.experimental import pallas as pl
from jax.experimental.pallas import tpu as pltpu
from jax.sharding import PartitionSpec as P

RADIUS = 4
POLICIES = 16
ROWS = 256
WIDTH = 1024
SUBS = 2
BLOCK = ROWS * SUBS
LOOP = 128
SEAM = 64
CHUNKS = 8
LINE = 8
MOVED = 2
LEVELS = 2 * RADIUS + 1
TURNS = 4
PIECES = 4
PART = ROWS // CHUNKS
SLOTS = (2 * RADIUS + 1) * SUBS
GROUP = 16
LOG2E = 1.4426950408889634
LN2 = 0.6931471805599453
LOWEST = -1e30
MESH = pl.DeviceIdType.MESH

OWN, HALF, FAR, SUB_FAR = 0, 2, 4, 6
CORE_NEAR_A, CORE_NEAR_B = 8, 10
SUB_OWN, CORE_OWN, CORE_HALF, CORE_FAR_A, CORE_FAR_B = 12, 13, 14, 15, 16
CLASSES = 17


def slot(offset, half):
    return (offset + RADIUS) * SUBS + half


def kernel(
    x_ref, reward_ref, partner_ref, policy_ref,
    weighted_ref, gradient_ref, loss_ref,
    keys, scores, level, rewards, integers, first_sum, second_sum,
    recv, send, level_sem, sum_sem, reward_sem, local_sem, word_sem,
):
    block = lax.axis_index("loop")
    sub = lax.axis_index("sub")
    core = lax.rem(block, 2)

    def crosses(at):
        return jnp.where(lax.rem(at, SEAM) >= SEAM - 2, 1, 0)

    def flip(half, by):
        return half + by - 2 * half * by

    def at_loop(index):
        return lax.rem(index + LOOP, LOOP)

    cross_up = crosses(block)
    cross_low = crosses(at_loop(block - 2))
    cross_up2 = crosses(at_loop(block + 2))
    cross_low2 = crosses(at_loop(block - 4))
    up_dev = (at_loop(block + 2), flip(sub, cross_up))
    low_dev = (at_loop(block - 2), flip(sub, cross_low))
    sub_dev = (block, 1 - sub)
    core_dev = (block + 1 - 2 * core, sub)
    low_half = flip(sub, cross_low)
    up_half = flip(sub, cross_up)
    low_far = flip(low_half, cross_low2)
    up_far = flip(up_half, cross_up2)

    own_slot = slot(0, sub)
    half_slot = slot(0, 1 - sub)

    def piece(index):
        return pl.ds(pl.multiple_of(index * ROWS, ROWS), ROWS)

    loads = [
        pltpu.make_async_copy(x_ref, keys.at[piece(own_slot)], local_sem.at[0]),
        pltpu.make_async_copy(reward_ref, rewards.at[sub], local_sem.at[1]),
        pltpu.make_async_copy(partner_ref, integers.at[0], local_sem.at[2]),
        pltpu.make_async_copy(policy_ref, integers.at[1], local_sem.at[3]),
    ]
    for load in loads:
        load.start()

    line = lax.rem(block, GROUP)
    line_base = block - line
    first_targets = [(line_base + lax.rem(line + i, GROUP), sub) for i in range(1, GROUP)]
    plane = (block // GROUP) * SUBS + sub
    x = lax.rem(block // GROUP, 4)
    y = (block // SEAM) * SUBS + sub
    steps = [(dx, dy) for dx in range(4) for dy in range(4) if dx or dy]
    steps.sort(key=lambda step: sum(min(d, 4 - d) for d in step))
    second_targets = []
    for dx, dy in steps:
        at_x, at_y = lax.rem(x + dx, 4), lax.rem(y + dy, 4)
        second_targets.append(
            ((at_y // SUBS) * SEAM + at_x * GROUP + line, lax.rem(at_y, SUBS))
        )
    barrier = pltpu.get_barrier_semaphore()
    x_base = block - lax.rem(block, SEAM)
    beside = [
        core_dev,
        sub_dev,
        (at_loop(block + SEAM), 1 - sub),
        (line_base + lax.rem(line + 2, GROUP), sub),
        (line_base + lax.rem(line + GROUP - 2, GROUP), sub),
        (x_base + lax.rem(block + GROUP, SEAM), sub),
        (x_base + lax.rem(block + SEAM - GROUP, SEAM), sub),
    ]
    greeted = [low_dev, up_dev] + beside
    for device in greeted:
        pl.semaphore_signal(barrier, inc=1, device_id=device, device_id_type=MESH)
    for load in loads:
        load.wait()
    pl.semaphore_wait(barrier, len(greeted))

    def tell(turn):
        for device in beside:
            pl.semaphore_signal(
                word_sem.at[turn], inc=1, device_id=device, device_id_type=MESH
            )

    def hear(turn):
        pl.semaphore_wait(word_sem.at[turn], len(beside))

    def rows(index, q):
        return pl.ds(pl.multiple_of(index * ROWS + q * PART, PART), PART)

    def push(source, target, kind, q, link, device):
        pltpu.make_async_remote_copy(
            src_ref=keys.at[rows(source, q)],
            dst_ref=keys.at[rows(target, q)],
            send_sem=send.at[link],
            recv_sem=recv.at[kind, q],
            device_id=device,
            device_id_type=MESH,
        ).start()

    def await_piece(kind, q):
        ref = keys.at[pl.ds(0, PART)]
        pltpu.make_async_copy(ref, ref, recv.at[kind, q]).wait()

    SUB, CORE = 2, 3
    shift = 2 * core - 1

    z = lax.rem(block // 2, LINE)
    side_b = jnp.where(z >= LINE // 2, 1, 0)
    side_a = 1 - side_b
    edge = jnp.where(jnp.logical_or(z < 2, z >= LINE - 2), 1, 0)

    def pick(side, low, up):
        return low + side * (up - low)

    def near(side):
        return 4 * side - 2

    def device_of(side):
        return tuple(pick(side, low, up) for low, up in zip(low_dev, up_dev))

    def near_half(side):
        return pick(side, low_half, up_half)

    def far_half_of(side):
        return pick(side, low_far, up_far)

    def to_core(offset, half, kind, q):
        push(slot(offset, half), slot(offset + shift, half), kind, q, CORE, core_dev)

    def send_own(side, *chunks):
        for q in chunks:
            push(own_slot, slot(-near(side), sub), OWN + 1 - side, q, side, device_of(side))

    def send_half(side, *chunks):
        for q in chunks:
            push(
                half_slot, slot(-near(side), 1 - sub), HALF + 1 - side, q, side,
                device_of(side),
            )

    def got_own(side, q):
        other = 1 - side
        await_piece(OWN + side, q)
        half = near_half(side)
        push(
            slot(near(side), half), slot(-2 * near(other), half), FAR + side, q, other,
            device_of(other),
        )

    def spread_own(side, q):
        to_core(near(side), near_half(side), CORE_NEAR_A + side, q)

    def got_half(q):
        await_piece(SUB_OWN, q)
        to_core(0, 1 - sub, CORE_HALF, q)

    far_offset = 4 - 8 * core
    far_half = far_half_of(1 - core)

    def got_far(side, q):
        await_piece(FAR + side, q)
        at = slot(2 * near(side), far_half_of(side))
        push(at, at, SUB_FAR + side, q, SUB, sub_dev)

    def spread_far(q):
        to_core(far_offset, far_half, CORE_FAR_A, q)

    def got_near(side, q):
        await_piece(HALF + side, q)
        to_core(near(side), 1 - near_half(side), CORE_NEAR_B + side, q)

    def got_sub(q):
        await_piece(SUB_FAR, q)
        await_piece(SUB_FAR + 1, q)
        to_core(far_offset, 1 - far_half, CORE_FAR_B, q)

    def await_all(kind):
        for q in range(CHUNKS):
            await_piece(kind, q)

    row_at = lax.broadcasted_iota(jnp.int32, (ROWS, ROWS), 0)
    column_at = lax.broadcasted_iota(jnp.int32, (ROWS, ROWS), 1)
    diagonal = row_at == column_at
    column_float = column_at.astype(jnp.float32)

    def as_column(row):
        return jnp.sum(jnp.where(diagonal, row, 0.0), axis=1, keepdims=True)

    def as_row(column):
        return jnp.sum(jnp.where(diagonal, column, 0.0), axis=0, keepdims=True)

    factor = LOG2E / math.sqrt(WIDTH)

    top = [None]
    total = [None]

    def absorb(index, part=None, own=False):
        absorb_all([index], part, own)

    def absorb_all(indices, part=None, own=False):
        first, count = (0, ROWS) if part is None else (part * 128, 128)
        parts = []
        width = ROWS // count
        for begin in range(0, len(indices), width):
            group = indices[begin : begin + width]
            wanted = [
                keys[pl.ds(pl.multiple_of(index * ROWS + first, 128), count), :]
                for index in group
            ]
            tile = lax.dot_general(
                keys[piece(own_slot), :], jnp.concatenate(wanted, axis=0),
                (((1,), (1,)), ((), ())), preferred_element_type=jnp.float32,
            ) * factor
            if own:
                tile = jnp.where(diagonal, LOWEST, tile)
            for place, index in enumerate(group):
                scores[index, :, first : first + count] = tile[:, place * count : (place + 1) * count]
            parts += [tile[:, i : i + 128] for i in range(0, len(group) * count, 128)]
        high = functools.reduce(jnp.maximum, parts)
        if top[0] is not None:
            high = jnp.maximum(high, top[0])
        fresh = functools.reduce(jnp.add, [jnp.exp2(t - high) for t in parts])
        if top[0] is not None:
            fresh = fresh + total[0] * jnp.exp2(top[0] - high)
        top[0], total[0] = high, fresh

    for q in range(4):
        send_own(side_a, q)
        send_own(side_b, q)
        push(own_slot, own_slot, SUB_OWN, q, SUB, sub_dev)

    @pl.when(edge == 1)
    def _():
        send_own(side_a, 4, 5)

    for q in range(4, CHUNKS):
        push(own_slot, own_slot, SUB_OWN, q, SUB, sub_dev)

    def near_a(q):
        got_own(side_a, q)
        if q < 4:
            send_own(side_b, q + 4)
        elif q < 7:
            send_half(side_b, q - 4)
        else:
            send_half(side_b, *range(3, CHUNKS - MOVED))

            @pl.when(z != 0)
            def _():
                send_half(side_b, *range(CHUNKS - MOVED, CHUNKS))
        spread_own(side_a, q)

    def near_b(q):
        got_own(side_b, q)
        if q < 2:
            send_own(side_a, q + 4 + 2 * edge)
        elif q < 4:

            @pl.when(edge == 1)
            def _():
                send_half(side_a, q - 2)

            @pl.when(edge == 0)
            def _():
                send_own(side_a, q + 4)
        else:
            send_half(side_a, q - 4 + 2 * edge)
        if q == 7:

            @pl.when(edge == 0)
            def _():
                send_half(side_a, 4, 5)

            send_half(side_a, 6, 7)
        if q >= CHUNKS - MOVED:
            at = slot(near(side_b), near_half(side_b))

            @pl.when(z == LINE - 1)
            def _():
                push(at, at, HALF + side_b, q, SUB, sub_dev)
        spread_own(side_b, q)

    def far_a(q):
        got_far(side_a, q)

    def far_b(q):
        got_far(side_b, q)
        spread_far(q)

    near_a(0)
    for q in range(CHUNKS):
        push(own_slot, slot(shift, sub), CORE_OWN, q, CORE, core_dev)
    reward_copy = pltpu.make_async_remote_copy(
        src_ref=rewards.at[sub], dst_ref=rewards.at[sub],
        send_sem=reward_sem.at[0], recv_sem=reward_sem.at[1],
        device_id=sub_dev, device_id_type=MESH,
    )
    reward_copy.start()
    near_a(1)
    tell(0)
    absorb(own_slot, own=True)
    near_a(2)
    near_b(0)
    near_a(3)
    near_b(1)
    far_a(0)
    for q in range(3):
        got_half(q)
    near_b(2)
    near_a(4)
    near_b(3)
    far_a(1)
    hear(0)
    tell(1)
    await_all(CORE_OWN)
    absorb(slot(-shift, sub))
    near_a(5)
    far_b(0)
    far_a(2)
    for q in range(3, CHUNKS):
        got_half(q)
    near_b(4)
    near_a(6)
    far_b(1)
    near_b(5)
    far_a(3)
    absorb(half_slot)
    near_a(7)
    far_b(2)
    hear(1)
    tell(2)
    near_b(6)
    far_a(4)
    reward_row = rewards[sub]
    reward_column = as_column(reward_row)
    partner_column = as_column((integers[0] - block * BLOCK).astype(jnp.float32))
    policy_column = as_column(integers[1].astype(jnp.float32))
    log_reward = jnp.log(reward_column) * LOG2E
    absorb(slot(near(side_a), near_half(side_a)))
    far_b(3)
    near_b(7)
    far_a(5)
    await_all(CORE_HALF)
    absorb(slot(-shift, 1 - sub))
    absorb(slot(near(side_b), near_half(side_b)))
    far_b(4)
    hear(2)
    tell(3)
    await_all(CORE_NEAR_A + side_a)
    absorb(slot(near(side_a) - shift, near_half(side_a)))
    far_a(6)
    await_all(CORE_NEAR_A + side_b)
    absorb(slot(near(side_b) - shift, near_half(side_b)))
    own_match = column_float + (sub * ROWS).astype(jnp.float32) == partner_column
    half_match = column_float + ((1 - sub) * ROWS).astype(jnp.float32) == partner_column
    positive = jnp.sum(
        jnp.where(own_match, scores[own_slot], 0.0)
        + jnp.where(half_match, scores[half_slot], 0.0),
        axis=1, keepdims=True,
    )
    far_b(5)
    absorb(slot(2 * near(side_a), far_half_of(side_a)), 0)
    far_a(7)
    absorb(slot(2 * near(side_b), far_half_of(side_b)), 0)
    for q in range(3):
        got_sub(q)
        got_near(side_a, q)
        got_near(side_b, q)
    far_b(6)
    hear(3)
    absorb(slot(2 * near(side_a), far_half_of(side_a)), 1)
    core_far = -far_offset - shift
    core_far_half = far_half_of(core)
    got_sub(3)
    got_near(side_a, 3)
    got_near(side_b, 3)
    far_b(7)

    def await_some(kind, part):
        for q in range(part * CHUNKS // 2, (part + 1) * CHUNKS // 2):
            await_piece(kind, q)

    def rest(part):
        sides = (side_a, side_b)
        absorb_all(
            [slot(near(side), 1 - near_half(side)) for side in sides]
            + [slot(2 * near(side), 1 - far_half_of(side)) for side in sides],
            part,
        )
        for side in sides:
            await_some(CORE_NEAR_B + side, part)
        await_some(CORE_FAR_B, part)
        absorb_all(
            [slot(near(side) - shift, 1 - near_half(side)) for side in sides]
            + [slot(core_far, 1 - core_far_half)],
            part,
        )

    rest(0)
    absorb(slot(2 * near(side_b), far_half_of(side_b)), 1)
    await_all(CORE_FAR_A)
    absorb(slot(core_far, core_far_half))
    for q in range(4, CHUNKS):
        got_near(side_a, q)
        got_near(side_b, q)
        got_sub(q)
    rest(1)

    peak = jnp.max(top[0], axis=1, keepdims=True)
    summed = jnp.sum(total[0] * jnp.exp2(top[0] - peak), axis=1, keepdims=True)
    log_total = peak + jnp.log(summed) * LOG2E
    own_level = log_total - log_reward
    level[own_slot] = as_row(own_level)
    toward_a = 2 * side_a - 1

    def send_level(offset, other):
        pltpu.make_async_remote_copy(
            src_ref=level.at[own_slot],
            dst_ref=level.at[slot(-offset, sub)],
            send_sem=level_sem.at[LEVELS],
            recv_sem=level_sem.at[RADIUS - offset],
            device_id=(at_loop(block + offset), flip(sub, other)),
            device_id_type=MESH,
        ).start()

    for k in range(RADIUS, 0, -1):
        for other in range(SUBS):
            send_level(-toward_a * k, other)
    weighted = reward_column * ((log_total - positive) * LN2)
    labels = lax.broadcasted_iota(jnp.int32, (ROWS, 128), 1).astype(jnp.float32)
    first_sum[line] = jnp.sum(
        jnp.where(labels == policy_column, weighted, 0.0), axis=0, keepdims=True
    )
    for device in first_targets:
        pltpu.make_async_remote_copy(
            src_ref=first_sum.at[line], dst_ref=first_sum.at[line],
            send_sem=sum_sem.at[0], recv_sem=sum_sem.at[1],
            device_id=device, device_id_type=MESH,
        ).start()
    for k in range(RADIUS, 0, -1):
        for other in range(SUBS):
            send_level(toward_a * k, other)
    send_level(0, 1)
    weighted_ref[...] = as_row(weighted)

    def await_rows(ref, count, sem):
        part = ref.at[pl.ds(0, count)]
        pltpu.make_async_copy(part, part, sem).wait()

    await_rows(first_sum, GROUP - 1, sum_sem.at[1])
    second_sum[plane] = jnp.sum(first_sum[...], axis=0)
    for device in second_targets:
        pltpu.make_async_remote_copy(
            src_ref=second_sum.at[plane], dst_ref=second_sum.at[plane],
            send_sem=sum_sem.at[2], recv_sem=sum_sem.at[3],
            device_id=device, device_id_type=MESH,
        ).start()
    reward_copy.wait()
    runs = (
        (-RADIUS * side_b, RADIUS + 1),
        (-RADIUS + (2 * RADIUS - 1) * side_b, 2),
        (-2 + 3 * side_b, 2),
    )
    for number, (begin, count) in enumerate(runs):
        for place in range(count):
            offset = begin + place
            if number == 0 and place in (0, RADIUS):

                @pl.when(offset == 0)
                def _():
                    await_rows(level, SUBS - 1, level_sem.at[RADIUS])

                @pl.when(offset != 0)
                def _():
                    await_rows(level, SUBS, level_sem.at[RADIUS + offset])
            else:
                await_rows(level, SUBS, level_sem.at[RADIUS + offset])
        values = []
        for place in range(count):
            offset = begin + place
            for half in range(SUBS):
                index = slot(offset, half)
                tile = scores[index]
                value = jnp.exp2(tile - own_level) + jnp.exp2(tile - level[index])
                if number == 0 and place in (0, RADIUS):
                    start = (offset * BLOCK + half * ROWS).astype(jnp.float32)
                    match = column_float + start == partner_column
                    value = value - jnp.where(match, reward_column + rewards[half], 0.0)
                values.append(value.astype(jnp.bfloat16))
        inner = pl.ds(pl.multiple_of(slot(begin, 0) * ROWS, BLOCK), count * BLOCK)
        product = jnp.dot(
            jnp.concatenate(values, axis=1), keys[inner, :],
            preferred_element_type=jnp.float32,
        )
        gradient_ref[...] = product if number == 0 else gradient_ref[...] + product

    await_rows(second_sum, GROUP - 1, sum_sem.at[3])
    loss = jnp.sum(second_sum[...], axis=0) * (POLICIES / (LOOP * BLOCK))
    loss_ref[...] = loss[:, :POLICIES]

    await_rows(level, SLOTS - 1, level_sem.at[LEVELS])
    await_rows(first_sum, GROUP - 1, sum_sem.at[0])
    await_rows(second_sum, GROUP - 1, sum_sem.at[2])
    def await_sent(link, count):
        part = keys.at[pl.ds(0, count)]
        pltpu.make_async_copy(part, part, send.at[link]).wait()

    moved = MOVED * PART
    await_sent(side_a, 3 * ROWS)
    await_sent(side_b, 3 * ROWS - moved)
    await_sent(SUB, 3 * ROWS)
    await_sent(CORE, 8 * ROWS)

    @pl.when(z != 0)
    def _():
        await_sent(side_b, moved)

    @pl.when(z == LINE - 1)
    def _():
        await_sent(SUB, moved)


def finish(a_ref, b_ref, c_ref, a_out, b_out, c_out, sems):
    step = ROWS // PIECES
    pairs = [(b_ref.at[r], b_out.at[r]) for r in (pl.ds(i * step, step) for i in range(PIECES))]
    pairs = [(a_ref, a_out), (c_ref, c_out)] + pairs
    copies = [pltpu.make_async_copy(p, q, sems.at[i]) for i, (p, q) in enumerate(pairs)]
    for copy in copies:
        copy.start()
    for copy in copies:
        copy.wait()


def body(embeddings, reward, partner, policy):
    vmem = pl.BlockSpec(memory_space=pltpu.VMEM)
    hbm = pl.BlockSpec(memory_space=pltpu.HBM)
    outs = (
        jax.ShapeDtypeStruct((1, ROWS), jnp.float32),
        jax.ShapeDtypeStruct((ROWS, WIDTH), jnp.float32),
        jax.ShapeDtypeStruct((1, POLICIES), jnp.float32),
    )
    results = pl.pallas_call(
        kernel,
        out_shape=outs,
        in_specs=[hbm, hbm, hbm, hbm],
        out_specs=(vmem, vmem, vmem),
        scratch_shapes=[
            pltpu.VMEM((SLOTS * ROWS, WIDTH), jnp.bfloat16),
            pltpu.VMEM((SLOTS, ROWS, ROWS), jnp.float32),
            pltpu.VMEM((SLOTS, 1, ROWS), jnp.float32),
            pltpu.VMEM((SUBS, 1, ROWS), jnp.float32),
            pltpu.VMEM((2, 1, ROWS), jnp.int32),
            pltpu.VMEM((GROUP, 1, 128), jnp.float32),
            pltpu.VMEM((GROUP, 1, 128), jnp.float32),
            pltpu.SemaphoreType.DMA((CLASSES, CHUNKS)),
            pltpu.SemaphoreType.DMA((4,)),
            pltpu.SemaphoreType.DMA((LEVELS + 1,)),
            pltpu.SemaphoreType.DMA((4,)),
            pltpu.SemaphoreType.DMA((2,)),
            pltpu.SemaphoreType.DMA((4,)),
            pltpu.SemaphoreType.REGULAR((TURNS,)),
        ],
        name="band",
        compiler_params=pltpu.CompilerParams(
            collective_id=0, has_side_effects=True, vmem_limit_bytes=48 * 2**20
        ),
    )(
        *(
            pltpu.with_memory_space_constraint(a, pltpu.HBM)
            for a in (
                embeddings, reward.reshape(1, ROWS), partner.reshape(1, ROWS), policy.reshape(1, ROWS)
            )
        )
    )
    weighted, gradient, loss = pl.pallas_call(
        finish,
        out_shape=outs,
        in_specs=[vmem, vmem, vmem],
        out_specs=(hbm, hbm, hbm),
        scratch_shapes=[pltpu.SemaphoreType.DMA((PIECES + 2,))],
        name="finish",
        compiler_params=pltpu.CompilerParams(vmem_limit_bytes=8 * 2**20),
    )(*results)
    return weighted.reshape(ROWS), gradient, loss.reshape(POLICIES)


def solution(mesh):
    rows = P(("loop", "sub"))
    matrix = P(("loop", "sub"), None)
    return jax.shard_map(
        body, mesh=mesh, in_specs=(matrix, rows, rows, rows),
        out_specs=(rows, matrix, P()), check_vma=False,
    )
```

```python
import functools
import math

import jax
import jax.numpy as jnp
from jax import lax
from jax.experimental import pallas as pl
from jax.experimental.pallas import tpu as pltpu
from jax.sharding import PartitionSpec as P

RADIUS = 4
POLICIES = 16
ROWS = 256
WIDTH = 1024
SUBS = 2
BLOCK = ROWS * SUBS
LOOP = 128
SEAM = 64
CHUNKS = 8
LINE = 8
MOVED = 1
LEVELS = 2 * RADIUS + 1
TURNS = 4
PIECES = 4
PART = ROWS // CHUNKS
SLOTS = (2 * RADIUS + 1) * SUBS
GROUP = 16
LOG2E = 1.4426950408889634
LN2 = 0.6931471805599453
LOWEST = -1e30
MESH = pl.DeviceIdType.MESH

OWN, HALF, FAR, SUB_FAR = 0, 2, 4, 6
CORE_NEAR_A, CORE_NEAR_B = 8, 10
SUB_OWN, CORE_OWN, CORE_HALF, CORE_FAR_A, CORE_FAR_B = 12, 13, 14, 15, 16
CLASSES = 17


def slot(offset, half):
    return (offset + RADIUS) * SUBS + half


def kernel(
    x_ref, reward_ref, partner_ref, policy_ref,
    weighted_ref, gradient_ref, loss_ref,
    keys, scores, level, rewards, integers, first_sum, second_sum,
    recv, send, level_sem, sum_sem, reward_sem, local_sem, word_sem,
):
    block = lax.axis_index("loop")
    sub = lax.axis_index("sub")
    core = lax.rem(block, 2)

    def crosses(at):
        return jnp.where(lax.rem(at, SEAM) >= SEAM - 2, 1, 0)

    def flip(half, by):
        return half + by - 2 * half * by

    def at_loop(index):
        return lax.rem(index + LOOP, LOOP)

    cross_up = crosses(block)
    cross_low = crosses(at_loop(block - 2))
    cross_up2 = crosses(at_loop(block + 2))
    cross_low2 = crosses(at_loop(block - 4))
    up_dev = (at_loop(block + 2), flip(sub, cross_up))
    low_dev = (at_loop(block - 2), flip(sub, cross_low))
    sub_dev = (block, 1 - sub)
    core_dev = (block + 1 - 2 * core, sub)
    low_half = flip(sub, cross_low)
    up_half = flip(sub, cross_up)
    low_far = flip(low_half, cross_low2)
    up_far = flip(up_half, cross_up2)

    own_slot = slot(0, sub)
    half_slot = slot(0, 1 - sub)

    def piece(index):
        return pl.ds(pl.multiple_of(index * ROWS, ROWS), ROWS)

    loads = [
        pltpu.make_async_copy(x_ref, keys.at[piece(own_slot)], local_sem.at[0]),
        pltpu.make_async_copy(reward_ref, rewards.at[sub], local_sem.at[1]),
        pltpu.make_async_copy(partner_ref, integers.at[0], local_sem.at[2]),
        pltpu.make_async_copy(policy_ref, integers.at[1], local_sem.at[3]),
    ]
    for load in loads:
        load.start()

    line = lax.rem(block, GROUP)
    line_base = block - line
    first_targets = [(line_base + lax.rem(line + i, GROUP), sub) for i in range(1, GROUP)]
    plane = (block // GROUP) * SUBS + sub
    x = lax.rem(block // GROUP, 4)
    y = (block // SEAM) * SUBS + sub
    steps = [(dx, dy) for dx in range(4) for dy in range(4) if dx or dy]
    steps.sort(key=lambda step: sum(min(d, 4 - d) for d in step))
    second_targets = []
    for dx, dy in steps:
        at_x, at_y = lax.rem(x + dx, 4), lax.rem(y + dy, 4)
        second_targets.append(
            ((at_y // SUBS) * SEAM + at_x * GROUP + line, lax.rem(at_y, SUBS))
        )
    barrier = pltpu.get_barrier_semaphore()
    x_base = block - lax.rem(block, SEAM)
    beside = [
        core_dev,
        sub_dev,
        (at_loop(block + SEAM), 1 - sub),
        (line_base + lax.rem(line + 2, GROUP), sub),
        (line_base + lax.rem(line + GROUP - 2, GROUP), sub),
        (x_base + lax.rem(block + GROUP, SEAM), sub),
        (x_base + lax.rem(block + SEAM - GROUP, SEAM), sub),
    ]
    greeted = [low_dev, up_dev] + beside
    for device in greeted:
        pl.semaphore_signal(barrier, inc=1, device_id=device, device_id_type=MESH)
    for load in loads:
        load.wait()
    pl.semaphore_wait(barrier, len(greeted))

    def tell(turn):
        for device in beside:
            pl.semaphore_signal(
                word_sem.at[turn], inc=1, device_id=device, device_id_type=MESH
            )

    def hear(turn):
        pl.semaphore_wait(word_sem.at[turn], len(beside))

    def rows(index, q):
        return pl.ds(pl.multiple_of(index * ROWS + q * PART, PART), PART)

    def push(source, target, kind, q, link, device):
        pltpu.make_async_remote_copy(
            src_ref=keys.at[rows(source, q)],
            dst_ref=keys.at[rows(target, q)],
            send_sem=send.at[link],
            recv_sem=recv.at[kind, q],
            device_id=device,
            device_id_type=MESH,
        ).start()

    def await_piece(kind, q):
        ref = keys.at[pl.ds(0, PART)]
        pltpu.make_async_copy(ref, ref, recv.at[kind, q]).wait()

    SUB, CORE = 2, 3
    shift = 2 * core - 1

    z = lax.rem(block // 2, LINE)
    side_b = jnp.where(z >= LINE // 2, 1, 0)
    side_a = 1 - side_b
    edge = jnp.where(jnp.logical_or(z < 2, z >= LINE - 2), 1, 0)

    def pick(side, low, up):
        return low + side * (up - low)

    def near(side):
        return 4 * side - 2

    def device_of(side):
        return tuple(pick(side, low, up) for low, up in zip(low_dev, up_dev))

    def near_half(side):
        return pick(side, low_half, up_half)

    def far_half_of(side):
        return pick(side, low_far, up_far)

    def to_core(offset, half, kind, q):
        push(slot(offset, half), slot(offset + shift, half), kind, q, CORE, core_dev)

    def send_own(side, *chunks):
        for q in chunks:
            push(own_slot, slot(-near(side), sub), OWN + 1 - side, q, side, device_of(side))

    def send_half(side, *chunks):
        for q in chunks:
            push(
                half_slot, slot(-near(side), 1 - sub), HALF + 1 - side, q, side,
                device_of(side),
            )

    def got_own(side, q):
        other = 1 - side
        await_piece(OWN + side, q)
        half = near_half(side)
        push(
            slot(near(side), half), slot(-2 * near(other), half), FAR + side, q, other,
            device_of(other),
        )

    def spread_own(side, q):
        to_core(near(side), near_half(side), CORE_NEAR_A + side, q)

    def got_half(q):
        await_piece(SUB_OWN, q)
        to_core(0, 1 - sub, CORE_HALF, q)

    far_offset = 4 - 8 * core
    far_half = far_half_of(1 - core)

    def got_far(side, q):
        await_piece(FAR + side, q)
        at = slot(2 * near(side), far_half_of(side))
        push(at, at, SUB_FAR + side, q, SUB, sub_dev)

    def spread_far(q):
        to_core(far_offset, far_half, CORE_FAR_A, q)

    def got_near(side, q):
        await_piece(HALF + side, q)
        to_core(near(side), 1 - near_half(side), CORE_NEAR_B + side, q)

    def got_sub(q):
        await_piece(SUB_FAR, q)
        await_piece(SUB_FAR + 1, q)
        to_core(far_offset, 1 - far_half, CORE_FAR_B, q)

    def await_all(kind):
        for q in range(CHUNKS):
            await_piece(kind, q)

    row_at = lax.broadcasted_iota(jnp.int32, (ROWS, ROWS), 0)
    column_at = lax.broadcasted_iota(jnp.int32, (ROWS, ROWS), 1)
    diagonal = row_at == column_at
    column_float = column_at.astype(jnp.float32)

    def as_column(row):
        return jnp.sum(jnp.where(diagonal, row, 0.0), axis=1, keepdims=True)

    def as_row(column):
        return jnp.sum(jnp.where(diagonal, column, 0.0), axis=0, keepdims=True)

    factor = LOG2E / math.sqrt(WIDTH)

    top = [None]
    total = [None]

    def absorb(index, part=None, own=False):
        absorb_all([index], part, own)

    def absorb_all(indices, part=None, own=False):
        first, count = (0, ROWS) if part is None else (part * 128, 128)
        parts = []
        width = ROWS // count
        for begin in range(0, len(indices), width):
            group = indices[begin : begin + width]
            wanted = [
                keys[pl.ds(pl.multiple_of(index * ROWS + first, 128), count), :]
                for index in group
            ]
            tile = lax.dot_general(
                keys[piece(own_slot), :], jnp.concatenate(wanted, axis=0),
                (((1,), (1,)), ((), ())), preferred_element_type=jnp.float32,
            ) * factor
            if own:
                tile = jnp.where(diagonal, LOWEST, tile)
            for place, index in enumerate(group):
                scores[index, :, first : first + count] = tile[:, place * count : (place + 1) * count]
            parts += [tile[:, i : i + 128] for i in range(0, len(group) * count, 128)]
        high = functools.reduce(jnp.maximum, parts)
        if top[0] is not None:
            high = jnp.maximum(high, top[0])
        fresh = functools.reduce(jnp.add, [jnp.exp2(t - high) for t in parts])
        if top[0] is not None:
            fresh = fresh + total[0] * jnp.exp2(top[0] - high)
        top[0], total[0] = high, fresh

    for q in range(4):
        send_own(side_a, q)
        send_own(side_b, q)
        push(own_slot, own_slot, SUB_OWN, q, SUB, sub_dev)

    @pl.when(edge == 1)
    def _():
        send_own(side_a, 4, 5)

    for q in range(4, CHUNKS):
        push(own_slot, own_slot, SUB_OWN, q, SUB, sub_dev)

    def near_a(q):
        got_own(side_a, q)
        if q < 4:
            send_own(side_b, q + 4)
        elif q < 7:
            send_half(side_b, q - 4)
        else:
            send_half(side_b, *range(3, CHUNKS - MOVED))

            @pl.when(z != 0)
            def _():
                send_half(side_b, *range(CHUNKS - MOVED, CHUNKS))
        spread_own(side_a, q)

    def near_b(q):
        got_own(side_b, q)
        if q < 2:
            send_own(side_a, q + 4 + 2 * edge)
        elif q < 4:

            @pl.when(edge == 1)
            def _():
                send_half(side_a, q - 2)

            @pl.when(edge == 0)
            def _():
                send_own(side_a, q + 4)
        else:
            send_half(side_a, q - 4 + 2 * edge)
        if q == 7:

            @pl.when(edge == 0)
            def _():
                send_half(side_a, 4, 5)

            send_half(side_a, 6, 7)
        if q >= CHUNKS - MOVED:
            at = slot(near(side_b), near_half(side_b))

            @pl.when(z == LINE - 1)
            def _():
                push(at, at, HALF + side_b, q, SUB, sub_dev)
        spread_own(side_b, q)

    def far_a(q):
        got_far(side_a, q)

    def far_b(q):
        got_far(side_b, q)
        spread_far(q)

    near_a(0)
    for q in range(CHUNKS):
        push(own_slot, slot(shift, sub), CORE_OWN, q, CORE, core_dev)
    reward_copy = pltpu.make_async_remote_copy(
        src_ref=rewards.at[sub], dst_ref=rewards.at[sub],
        send_sem=reward_sem.at[0], recv_sem=reward_sem.at[1],
        device_id=sub_dev, device_id_type=MESH,
    )
    reward_copy.start()
    near_a(1)
    tell(0)
    absorb(own_slot, own=True)
    near_a(2)
    near_b(0)
    near_a(3)
    near_b(1)
    far_a(0)
    for q in range(3):
        got_half(q)
    near_b(2)
    near_a(4)
    near_b(3)
    far_a(1)
    hear(0)
    tell(1)
    await_all(CORE_OWN)
    absorb(slot(-shift, sub))
    near_a(5)
    far_b(0)
    far_a(2)
    for q in range(3, CHUNKS):
        got_half(q)
    near_b(4)
    near_a(6)
    far_b(1)
    near_b(5)
    far_a(3)
    absorb(half_slot)
    near_a(7)
    far_b(2)
    hear(1)
    tell(2)
    near_b(6)
    far_a(4)
    reward_row = rewards[sub]
    reward_column = as_column(reward_row)
    partner_column = as_column((integers[0] - block * BLOCK).astype(jnp.float32))
    policy_column = as_column(integers[1].astype(jnp.float32))
    log_reward = jnp.log(reward_column) * LOG2E
    absorb(slot(near(side_a), near_half(side_a)))
    far_b(3)
    near_b(7)
    far_a(5)
    await_all(CORE_HALF)
    absorb(slot(-shift, 1 - sub))
    absorb(slot(near(side_b), near_half(side_b)))
    far_b(4)
    hear(2)
    tell(3)
    await_all(CORE_NEAR_A + side_a)
    absorb(slot(near(side_a) - shift, near_half(side_a)))
    far_a(6)
    await_all(CORE_NEAR_A + side_b)
    absorb(slot(near(side_b) - shift, near_half(side_b)))
    own_match = column_float + (sub * ROWS).astype(jnp.float32) == partner_column
    half_match = column_float + ((1 - sub) * ROWS).astype(jnp.float32) == partner_column
    positive = jnp.sum(
        jnp.where(own_match, scores[own_slot], 0.0)
        + jnp.where(half_match, scores[half_slot], 0.0),
        axis=1, keepdims=True,
    )
    far_b(5)
    absorb(slot(2 * near(side_a), far_half_of(side_a)), 0)
    far_a(7)
    absorb(slot(2 * near(side_b), far_half_of(side_b)), 0)
    for q in range(3):
        got_sub(q)
        got_near(side_a, q)
        got_near(side_b, q)
    far_b(6)
    hear(3)
    absorb(slot(2 * near(side_a), far_half_of(side_a)), 1)
    core_far = -far_offset - shift
    core_far_half = far_half_of(core)
    got_sub(3)
    got_near(side_a, 3)
    got_near(side_b, 3)
    far_b(7)

    def await_some(kind, part):
        for q in range(part * CHUNKS // 2, (part + 1) * CHUNKS // 2):
            await_piece(kind, q)

    def rest(part):
        sides = (side_a, side_b)
        absorb_all(
            [slot(near(side), 1 - near_half(side)) for side in sides]
            + [slot(2 * near(side), 1 - far_half_of(side)) for side in sides],
            part,
        )
        for side in sides:
            await_some(CORE_NEAR_B + side, part)
        await_some(CORE_FAR_B, part)
        absorb_all(
            [slot(near(side) - shift, 1 - near_half(side)) for side in sides]
            + [slot(core_far, 1 - core_far_half)],
            part,
        )

    rest(0)
    absorb(slot(2 * near(side_b), far_half_of(side_b)), 1)
    await_all(CORE_FAR_A)
    absorb(slot(core_far, core_far_half))
    for q in range(4, CHUNKS):
        got_near(side_a, q)
        got_near(side_b, q)
        got_sub(q)
    rest(1)

    peak = jnp.max(top[0], axis=1, keepdims=True)
    summed = jnp.sum(total[0] * jnp.exp2(top[0] - peak), axis=1, keepdims=True)
    log_total = peak + jnp.log(summed) * LOG2E
    own_level = log_total - log_reward
    level[own_slot] = as_row(own_level)
    toward_a = 2 * side_a - 1

    def send_level(offset, other):
        pltpu.make_async_remote_copy(
            src_ref=level.at[own_slot],
            dst_ref=level.at[slot(-offset, sub)],
            send_sem=level_sem.at[LEVELS],
            recv_sem=level_sem.at[RADIUS - offset],
            device_id=(at_loop(block + offset), flip(sub, other)),
            device_id_type=MESH,
        ).start()

    for k in range(RADIUS, 0, -1):
        for other in range(SUBS):
            send_level(-toward_a * k, other)
    weighted = reward_column * ((log_total - positive) * LN2)
    labels = lax.broadcasted_iota(jnp.int32, (ROWS, 128), 1).astype(jnp.float32)
    first_sum[line] = jnp.sum(
        jnp.where(labels == policy_column, weighted, 0.0), axis=0, keepdims=True
    )
    for device in first_targets:
        pltpu.make_async_remote_copy(
            src_ref=first_sum.at[line], dst_ref=first_sum.at[line],
            send_sem=sum_sem.at[0], recv_sem=sum_sem.at[1],
            device_id=device, device_id_type=MESH,
        ).start()
    for k in range(RADIUS, 0, -1):
        for other in range(SUBS):
            send_level(toward_a * k, other)
    send_level(0, 1)
    weighted_ref[...] = as_row(weighted)

    def await_rows(ref, count, sem):
        part = ref.at[pl.ds(0, count)]
        pltpu.make_async_copy(part, part, sem).wait()

    await_rows(first_sum, GROUP - 1, sum_sem.at[1])
    second_sum[plane] = jnp.sum(first_sum[...], axis=0)
    for device in second_targets:
        pltpu.make_async_remote_copy(
            src_ref=second_sum.at[plane], dst_ref=second_sum.at[plane],
            send_sem=sum_sem.at[2], recv_sem=sum_sem.at[3],
            device_id=device, device_id_type=MESH,
        ).start()
    reward_copy.wait()
    runs = (
        (-RADIUS * side_b, RADIUS + 1),
        (-RADIUS + (2 * RADIUS - 1) * side_b, 2),
        (-2 + 3 * side_b, 2),
    )
    for number, (begin, count) in enumerate(runs):
        for place in range(count):
            offset = begin + place
            if number == 0 and place in (0, RADIUS):

                @pl.when(offset == 0)
                def _():
                    await_rows(level, SUBS - 1, level_sem.at[RADIUS])

                @pl.when(offset != 0)
                def _():
                    await_rows(level, SUBS, level_sem.at[RADIUS + offset])
            else:
                await_rows(level, SUBS, level_sem.at[RADIUS + offset])
        values = []
        for place in range(count):
            offset = begin + place
            for half in range(SUBS):
                index = slot(offset, half)
                tile = scores[index]
                value = jnp.exp2(tile - own_level) + jnp.exp2(tile - level[index])
                if number == 0 and place in (0, RADIUS):
                    start = (offset * BLOCK + half * ROWS).astype(jnp.float32)
                    match = column_float + start == partner_column
                    value = value - jnp.where(match, reward_column + rewards[half], 0.0)
                values.append(value.astype(jnp.bfloat16))
        inner = pl.ds(pl.multiple_of(slot(begin, 0) * ROWS, BLOCK), count * BLOCK)
        product = jnp.dot(
            jnp.concatenate(values, axis=1), keys[inner, :],
            preferred_element_type=jnp.float32,
        )
        gradient_ref[...] = product if number == 0 else gradient_ref[...] + product

    await_rows(second_sum, GROUP - 1, sum_sem.at[3])
    loss = jnp.sum(second_sum[...], axis=0) * (POLICIES / (LOOP * BLOCK))
    loss_ref[...] = loss[:, :POLICIES]

    await_rows(level, SLOTS - 1, level_sem.at[LEVELS])
    await_rows(first_sum, GROUP - 1, sum_sem.at[0])
    await_rows(second_sum, GROUP - 1, sum_sem.at[2])
    def await_sent(link, count):
        part = keys.at[pl.ds(0, count)]
        pltpu.make_async_copy(part, part, send.at[link]).wait()

    moved = MOVED * PART
    await_sent(side_a, 3 * ROWS)
    await_sent(side_b, 3 * ROWS - moved)
    await_sent(SUB, 3 * ROWS)
    await_sent(CORE, 8 * ROWS)

    @pl.when(z != 0)
    def _():
        await_sent(side_b, moved)

    @pl.when(z == LINE - 1)
    def _():
        await_sent(SUB, moved)


def finish(a_ref, b_ref, c_ref, a_out, b_out, c_out, sems):
    step = ROWS // PIECES
    pairs = [(b_ref.at[r], b_out.at[r]) for r in (pl.ds(i * step, step) for i in range(PIECES))]
    pairs = [(a_ref, a_out), (c_ref, c_out)] + pairs
    copies = [pltpu.make_async_copy(p, q, sems.at[i]) for i, (p, q) in enumerate(pairs)]
    for copy in copies:
        copy.start()
    for copy in copies:
        copy.wait()


def body(embeddings, reward, partner, policy):
    vmem = pl.BlockSpec(memory_space=pltpu.VMEM)
    hbm = pl.BlockSpec(memory_space=pltpu.HBM)
    outs = (
        jax.ShapeDtypeStruct((1, ROWS), jnp.float32),
        jax.ShapeDtypeStruct((ROWS, WIDTH), jnp.float32),
        jax.ShapeDtypeStruct((1, POLICIES), jnp.float32),
    )
    results = pl.pallas_call(
        kernel,
        out_shape=outs,
        in_specs=[hbm, hbm, hbm, hbm],
        out_specs=(vmem, vmem, vmem),
        scratch_shapes=[
            pltpu.VMEM((SLOTS * ROWS, WIDTH), jnp.bfloat16),
            pltpu.VMEM((SLOTS, ROWS, ROWS), jnp.float32),
            pltpu.VMEM((SLOTS, 1, ROWS), jnp.float32),
            pltpu.VMEM((SUBS, 1, ROWS), jnp.float32),
            pltpu.VMEM((2, 1, ROWS), jnp.int32),
            pltpu.VMEM((GROUP, 1, 128), jnp.float32),
            pltpu.VMEM((GROUP, 1, 128), jnp.float32),
            pltpu.SemaphoreType.DMA((CLASSES, CHUNKS)),
            pltpu.SemaphoreType.DMA((4,)),
            pltpu.SemaphoreType.DMA((LEVELS + 1,)),
            pltpu.SemaphoreType.DMA((4,)),
            pltpu.SemaphoreType.DMA((2,)),
            pltpu.SemaphoreType.DMA((4,)),
            pltpu.SemaphoreType.REGULAR((TURNS,)),
        ],
        name="band",
        compiler_params=pltpu.CompilerParams(
            collective_id=0, has_side_effects=True, vmem_limit_bytes=48 * 2**20
        ),
    )(
        *(
            pltpu.with_memory_space_constraint(a, pltpu.HBM)
            for a in (
                embeddings, reward.reshape(1, ROWS), partner.reshape(1, ROWS), policy.reshape(1, ROWS)
            )
        )
    )
    weighted, gradient, loss = pl.pallas_call(
        finish,
        out_shape=outs,
        in_specs=[vmem, vmem, vmem],
        out_specs=(hbm, hbm, hbm),
        scratch_shapes=[pltpu.SemaphoreType.DMA((PIECES + 2,))],
        name="finish",
        compiler_params=pltpu.CompilerParams(vmem_limit_bytes=8 * 2**20),
    )(*results)
    return weighted.reshape(ROWS), gradient, loss.reshape(POLICIES)


def solution(mesh):
    rows = P(("loop", "sub"))
    matrix = P(("loop", "sub"), None)
    return jax.shard_map(
        body, mesh=mesh, in_specs=(matrix, rows, rows, rows),
        out_specs=(rows, matrix, P()), check_vma=False,
    )
```
